32 devices in a mesh: row: 2 (over x), col: 16 (over z, y, core).
Axes of the slice: x: 2, y: 2, z: 4, core: 2. Of those that a mesh axis runs over, the one named last changes fastest.
Arguments:
- amplitudes: bfloat16 [2048, 65536], P('row', 'col'), may hold values from -6 to 6
- residual_in: bfloat16 [2048, 65536], P('row', 'col'), may hold values from -6 to 6
- cholesky: bfloat16 [65536, 1280], P('col', 'row'), may hold values from -0.0625 to 0.0625
Outputs:
- residual_out: bfloat16 [2048, 65536], P('row', 'col')
The draws below stay inside these ranges and needn't reach their ends.
All inputs are finite; a program needn't handle non-finite values.
Results may differ from the reference program's by a relative error of at most 0.004.
Values may be sent and summed in bfloat16 or wider, within the bound.
No kernel may reach another device: no remote copies, remote signals or barrier semaphores. Data moves between devices by JAX's collectives and lax.ppermute only.
A program may use at most 128 MiB of HBM per device.

```python
import jax
import jax.numpy as jnp
from jax import lax

JB = 65536
NVEC = 1280
ROWS = 2048


def block_scale(own_key, extent, cuts, low, top_value):
    gain = 1.0
    for dim, shards_of in cuts:
        draws = jax.random.uniform(jax.random.fold_in(jax.random.fold_in(own_key, 6), dim), (shards_of,), jnp.float32, low / len(cuts), top_value / len(cuts))
        gain = gain * jnp.repeat(jnp.exp(draws), extent[dim] // shards_of).reshape((-1,) + (1,) * (len(extent) - 1 - dim))
    return gain


def gaussian(key, dims, deviation, reach, pieces=(), kind=jnp.bfloat16):
    values = deviation * jax.random.normal(key, dims, jnp.float32)
    if pieces:
        values = values * block_scale(key, dims, pieces, -0.22, 0.18)
    return jnp.clip(values, -reach, reach).astype(kind)


def setup_inputs(seed: int = 0) -> dict:
    key_of = jax.random.split(jax.random.key(seed), 4)
    amplitudes = gaussian(key_of[0], (ROWS, JB), 1.0, 6.0, ((0, 2), (1, 16)))
    residual_in = gaussian(key_of[1], (ROWS, JB), 1.0, 6.0, ((0, 2), (1, 16)))
    cholesky = gaussian(key_of[2], (JB, NVEC), (JB // 8) ** -0.5, 0.0625, ((0, 16), (1, 2)))
    return {"amplitudes": amplitudes, "residual_in": residual_in, "cholesky": cholesky}


def reference(amplitudes, residual_in, cholesky):
    chi_sum = jnp.dot(amplitudes, cholesky, preferred_element_type=jnp.float32)
    chi = chi_sum.astype(jnp.bfloat16)
    update = lax.dot_general(chi, cholesky, (((1,), (1,)), ((), ())), preferred_element_type=jnp.float32)
    return (residual_in.astype(jnp.float32) + update).astype(jnp.bfloat16)
```

```python
import jax
import jax.numpy as jnp
from jax import lax
from jax.experimental import pallas as pl
from jax.experimental.layout import Layout, with_layout_constraint
from jax.experimental.pallas import tpu as pltpu
from jax.sharding import PartitionSpec as P

GROUPS = (128, 256, 256)
VMEM_BYTES = 30 * 1024 * 1024


def after(value, *others):
    return lax.optimization_barrier((value, *others))[0]


def block_of(extent, target):
    while extent % target:
        target //= 2
    return target


def project(amplitudes, vectors):
    part = jnp.dot(amplitudes, vectors, preferred_element_type=jnp.float32)
    return with_layout_constraint(part, Layout(major_to_minor=(0, 1)))


def project_back(base, groups, kind):
    rows, columns = base.shape
    block = block_of(columns, 1024)
    chis = [chi for chi, _ in groups]
    pieces = [piece for _, members in groups for piece in members]

    def kernel(base_ref, *refs):
        left = jnp.concatenate([c[...] for c in refs[: len(chis)]], axis=1)
        right = jnp.concatenate([p[...] for p in refs[len(chis) : -1]], axis=1)
        term = lax.dot_general(left, right, (((1,), (1,)), ((), ())), preferred_element_type=jnp.float32)
        refs[-1][...] = (base_ref[...].astype(jnp.float32) + term).astype(kind)

    return pl.pallas_call(
        kernel,
        grid=(columns // block,),
        in_specs=[pl.BlockSpec((rows, block), lambda i: (0, i))]
        + [pl.BlockSpec(chi.shape, lambda i: (0, 0), pipeline_mode=pl.Buffered(1)) for chi in chis]
        + [pl.BlockSpec((block, piece.shape[1]), lambda i: (i, 0)) for piece in pieces],
        out_specs=pl.BlockSpec((rows, block), lambda i: (0, i)),
        out_shape=jax.ShapeDtypeStruct(base.shape, kind),
        compiler_params=pltpu.CompilerParams(vmem_limit_bytes=VMEM_BYTES),
        cost_estimate=pl.CostEstimate(flops=0, bytes_accessed=0, transcendentals=0),
    )(base, *chis, *pieces)


def solution(mesh):
    rows, cols = mesh.shape["row"], mesh.shape["col"]
    bits = [1 << k for k in range(cols.bit_length() - 1)]

    def exchange(value, bit):
        return lax.ppermute(value, "col", [(i, i ^ bit) for i in range(cols)])

    def body(amplitudes, residual_in, cholesky):
        me = lax.axis_index("col")
        upper = [(me & bit) != 0 for bit in bits]
        once = 1 + (me >> 20)

        def boxed(run, *values):
            shapes = jax.eval_shape(run, *values)
            zeros = jax.tree.map(lambda s: jnp.zeros(s.shape, s.dtype), shapes)
            return lax.while_loop(lambda s: s[0] < once, lambda s: (s[0] + 1, run(*values)), (jnp.int32(0), zeros))[1]

        def halve(value, step, narrow):
            half = value.shape[0] // 2
            low, high = value[:half], value[half:]
            send = jnp.where(upper[step], low, high)
            got = exchange(send.astype(narrow) if step else send, bits[step])
            return jnp.where(upper[step], high, low) + got.astype(jnp.float32)

        def double(value, step):
            up = upper[step]
            got = exchange(value, bits[step])
            return jnp.concatenate([jnp.where(up, got, value), jnp.where(up, value, got)])

        steps = range(len(bits))

        def scatter(value, narrow=jnp.float32):
            for step in steps:
                value = halve(value, step, narrow)
            return value.astype(jnp.bfloat16)

        def gather(value):
            for step in steps[::-1]:
                value = double(value, step)
            return value

        def send_row(vectors, shift):
            return lax.ppermute(vectors, "row", [(i, (i + shift) % rows) for i in range(rows)])

        if rows != 2 or len(bits) != 4 or sum(GROUPS) != cholesky.shape[1]:
            rest = jnp.concatenate([send_row(cholesky, shift) for shift in range(1, rows)], axis=1)
            chi = gather(scatter(project(amplitudes, cholesky)))
            total = project_back(residual_in, [(chi, [cholesky])], jnp.float32)
            rest = after(rest, total)
            return project_back(total, [(gather(scatter(project(amplitudes, rest))), [rest])], jnp.bfloat16)

        ends = [sum(GROUPS[: k + 1]) for k in range(len(GROUPS))]
        out_a, out_b, out_c = [cholesky[:, end - size : end] for end, size in zip(ends, GROUPS)]
        a = send_row(out_a, 1)
        part_own = project(amplitudes, after(cholesky, out_a))
        own = lax.psum_scatter(part_own, "col", scatter_dimension=0, tiled=True).astype(jnp.bfloat16)
        b = send_row(after(out_b, part_own), 1)
        part_a = project(amplitudes, after(a, part_own))
        chi_a = boxed(lambda v: gather(scatter(v)), part_a)
        c = send_row(after(out_c, chi_a), 1)
        part_b = project(amplitudes, after(b, chi_a))
        own = after(own, part_b)
        chi_own = lax.all_gather(own, "col", axis=0, tiled=True)
        chi_b = boxed(lambda v: gather(scatter(v)), after(part_b, own))
        chi_c = gather(scatter(project(amplitudes, after(c, chi_b, chi_own)), jnp.bfloat16))
        groups = [(chi_own, [cholesky]), (chi_a, [a]), (chi_b, [b]), (chi_c, [c])]
        return project_back(residual_in, groups, jnp.bfloat16)

    in_specs = (P("row", "col"), P("row", "col"), P("col", "row"))
    return jax.shard_map(body, mesh=mesh, in_specs=in_specs, out_specs=P("row", "col"), check_vma=False)
```

```python
import jax
import jax.numpy as jnp
from jax import lax
from jax.experimental import pallas as pl
from jax.experimental.layout import Layout, with_layout_constraint
from jax.experimental.pallas import tpu as pltpu
from jax.sharding import PartitionSpec as P

GROUPS = (128, 256, 256)
KINDS = (jnp.float32, jnp.bfloat16, jnp.bfloat16)
TURN = 1
VMEM_BYTES = 58 * 1024 * 1024


def after(value, *others):
    return lax.optimization_barrier((value, *others))[0]


def block_of(extent, target):
    while extent % target:
        target //= 2
    return target


def project(amplitudes, vectors):
    part = jnp.dot(amplitudes, vectors, preferred_element_type=jnp.float32)
    return with_layout_constraint(part, Layout(major_to_minor=(0, 1)))


def project_back(base, groups, kind):
    rows, columns = base.shape
    block = block_of(columns, 1024)
    chis = [chi for chi, _ in groups]
    pieces = [piece for _, members in groups for piece in members]

    def kernel(base_ref, *refs):
        left = jnp.concatenate([c[...] for c in refs[: len(chis)]], axis=1)
        right = jnp.concatenate([p[...] for p in refs[len(chis) : -1]], axis=1)
        term = lax.dot_general(left, right, (((1,), (1,)), ((), ())), preferred_element_type=jnp.float32)
        refs[-1][...] = (base_ref[...].astype(jnp.float32) + term).astype(kind)

    return pl.pallas_call(
        kernel,
        grid=(columns // block,),
        in_specs=[pl.BlockSpec((rows, block), lambda i: (0, i))]
        + [pl.BlockSpec(chi.shape, lambda i: (0, 0), pipeline_mode=pl.Buffered(1)) for chi in chis]
        + [pl.BlockSpec((block, piece.shape[1]), lambda i: (i, 0)) for piece in pieces],
        out_specs=pl.BlockSpec((rows, block), lambda i: (0, i)),
        out_shape=jax.ShapeDtypeStruct(base.shape, kind),
        compiler_params=pltpu.CompilerParams(vmem_limit_bytes=VMEM_BYTES),
        cost_estimate=pl.CostEstimate(flops=0, bytes_accessed=0, transcendentals=0),
    )(base, *chis, *pieces)


def solution(mesh):
    rows, cols = mesh.shape["row"], mesh.shape["col"]

    def exchange(value, bit):
        return lax.ppermute(value, "col", [(i, i ^ bit) for i in range(cols)])

    def body(amplitudes, residual_in, cholesky):
        me = lax.axis_index("col")
        once = 1 + (me >> 20)

        def boxed(run, *values):
            shapes = jax.eval_shape(run, *values)
            zeros = jax.tree.map(lambda s: jnp.zeros(s.shape, s.dtype), shapes)

            def trip(state):
                return state[0] + 1, run(*[after(value, state[0]) for value in values])

            return lax.while_loop(lambda state: state[0] < once, trip, (jnp.int32(0), zeros))[1]

        bits = [1 << k for k in range(cols.bit_length() - 1)]
        upper = [(me & bit) != 0 for bit in bits]

        def halve(value, step, kind):
            half = value.shape[0] // 2
            low, high = value[:half], value[half:]
            got = exchange(jnp.where(upper[step], low, high).astype(kind), bits[step])
            return jnp.where(upper[step], high, low) + got.astype(jnp.float32)

        def double(value, step):
            got = exchange(value, bits[step])
            return jnp.concatenate([jnp.where(upper[step], got, value), jnp.where(upper[step], value, got)])

        mates = [[i for i in range(cols) if i % 2 == core] for core in range(2)]
        count = cols // 2

        def spread(value):
            return lax.all_to_all(value, "col", 0, 0, tiled=True, axis_index_groups=mates)

        def scatter(value, kind=jnp.float32):
            value = halve(value, 0, jnp.float32)
            parts = spread(value.astype(kind)).astype(jnp.float32)
            return jnp.sum(parts.reshape(count, parts.shape[0] // count, -1), axis=0).astype(jnp.bfloat16)

        def gather(value):
            return spread(jnp.tile(value, (count, 1)))

        def send_row(vectors, shift):
            return lax.ppermute(vectors, "row", [(i, (i + shift) % rows) for i in range(rows)])

        if rows != 2 or sum(GROUPS) != cholesky.shape[1]:
            rest = jnp.concatenate([send_row(cholesky, shift) for shift in range(1, rows)], axis=1)
            chi = double(gather(scatter(project(amplitudes, cholesky))), 0)
            total = project_back(residual_in, [(chi, [cholesky])], jnp.float32)
            rest = after(rest, total)
            chi = double(gather(scatter(project(amplitudes, rest))), 0)
            return project_back(total, [(chi, [rest])], jnp.bfloat16)

        ends = [sum(GROUPS[: k + 1]) for k in range(len(GROUPS))]
        outs = [cholesky[:, end - size : end] for end, size in zip(ends, GROUPS)]
        pieces = [send_row(outs[0], 1)]
        part = project(amplitudes, after(cholesky, outs[0]))
        pieces.append(send_row(after(outs[1], part), 1))
        own = lax.psum_scatter(part, "col", scatter_dimension=0, tiled=True).astype(jnp.bfloat16)
        groups = []
        waits = [part]
        for k, kind in enumerate(KINDS):
            part = project(amplitudes, after(pieces[k], *waits))
            if k == TURN:
                own = after(own, part)
                chi_own = lax.all_gather(own, "col", axis=0, tiled=True)
                part = after(part, own)
            if k < len(GROUPS) - 1:
                chi = double(boxed(lambda v: gather(scatter(v, kind)), part), 0)
            else:
                chi = double(gather(scatter(part, kind)), 0)
            if len(pieces) < len(GROUPS):
                pieces.append(send_row(after(outs[len(pieces)], chi), 1))
            waits = [chi] if k + 2 < len(GROUPS) else [chi, chi_own]
            groups.append((chi, [pieces[k]]))
        return project_back(residual_in, [(chi_own, [cholesky])] + groups, jnp.bfloat16)

    in_specs = (P("row", "col"), P("row", "col"), P("col", "row"))
    return jax.shard_map(body, mesh=mesh, in_specs=in_specs, out_specs=P("row", "col"), check_vma=False)
```

```python
import jax
import jax.numpy as jnp
from jax import lax
from jax.experimental import pallas as pl
from jax.experimental.layout import Layout, with_layout_constraint
from jax.experimental.pallas import tpu as pltpu
from jax.sharding import PartitionSpec as P

GROUPS = (128, 256, 256)
VMEM_BYTES = 58 * 1024 * 1024
FREE = pl.CostEstimate(flops=0, bytes_accessed=0, transcendentals=0)


def after(value, *others):
    return lax.optimization_barrier((value, *others))[0]


def block_of(extent, target):
    while extent % target:
        target //= 2
    return target


def project(amplitudes, vectors):
    part = jnp.dot(amplitudes, vectors, preferred_element_type=jnp.float32)
    return with_layout_constraint(part, Layout(major_to_minor=(0, 1)))


def project_wide(amplitudes, vectors):
    rows, depth = amplitudes.shape
    width = vectors.shape[1]
    block = block_of(depth, 1024)
    steps = depth // block

    def kernel(left_ref, right_ref, out_ref, total_ref):
        step = pl.program_id(0)
        term = lax.dot_general(right_ref[...].T, left_ref[...], (((1,), (1,)), ((), ())), preferred_element_type=jnp.float32)

        @pl.when(step == 0)
        def _():
            total_ref[...] = term

        @pl.when((step > 0) & (step < steps - 1))
        def _():
            total_ref[...] += term

        @pl.when(step == steps - 1)
        def _():
            out_ref[...] = (total_ref[...] + term).T

    return pl.pallas_call(
        kernel,
        grid=(steps,),
        in_specs=[pl.BlockSpec((rows, block), lambda k: (0, k)), pl.BlockSpec((block, width), lambda k: (k, 0))],
        out_specs=pl.BlockSpec((rows, width), lambda k: (0, 0)),
        out_shape=jax.ShapeDtypeStruct((rows, width), jnp.float32),
        scratch_shapes=[pltpu.VMEM((width, rows), jnp.float32)],
        compiler_params=pltpu.CompilerParams(vmem_limit_bytes=VMEM_BYTES),
        cost_estimate=FREE,
    )(amplitudes, vectors)


def project_back(base, chis, pieces, kind):
    rows, columns = base.shape
    block = block_of(columns, 1024)

    def kernel(base_ref, *refs):
        left = jnp.concatenate([c[...] for c in refs[: len(chis)]], axis=1)
        right = jnp.concatenate([p[...] for p in refs[len(chis) : -1]], axis=1)
        term = lax.dot_general(left, right, (((1,), (1,)), ((), ())), preferred_element_type=jnp.float32)
        refs[-1][...] = (base_ref[...].astype(jnp.float32) + term).astype(kind)

    return pl.pallas_call(
        kernel,
        grid=(columns // block,),
        in_specs=[pl.BlockSpec((rows, block), lambda i: (0, i))]
        + [pl.BlockSpec(chi.shape, lambda i: (0, 0), pipeline_mode=pl.Buffered(1)) for chi in chis]
        + [pl.BlockSpec((block, piece.shape[1]), lambda i: (i, 0)) for piece in pieces],
        out_specs=pl.BlockSpec((rows, block), lambda i: (0, i)),
        out_shape=jax.ShapeDtypeStruct(base.shape, kind),
        compiler_params=pltpu.CompilerParams(vmem_limit_bytes=VMEM_BYTES),
        cost_estimate=FREE,
    )(base, *chis, *pieces)


def solution(mesh):
    rows, cols = mesh.shape["row"], mesh.shape["col"]

    def exchange(value, bit):
        return lax.ppermute(value, "col", [(i, i ^ bit) for i in range(cols)])

    def body(amplitudes, residual_in, cholesky):
        me = lax.axis_index("col")
        once = 1 + (me >> 20)

        def boxed(run, *values):
            shapes = jax.eval_shape(run, *values)
            zeros = jax.tree.map(lambda s: jnp.zeros(s.shape, s.dtype), shapes)

            def trip(state):
                return state[0] + 1, run(*[after(value, state[0]) for value in values])

            return lax.while_loop(lambda state: state[0] < once, trip, (jnp.int32(0), zeros))[1]

        bits = [1 << k for k in range(cols.bit_length() - 1)]
        upper = [(me & bit) != 0 for bit in bits]

        def split(value, step):
            low, high = jnp.split(value, 2)
            return jnp.where(upper[step], high, low), jnp.where(upper[step], low, high)

        def halve(value, step, kind):
            keep, send = split(value, step)
            return keep + exchange(send.astype(kind), bits[step]).astype(jnp.float32)

        def double(value, step):
            got = exchange(value, bits[step])
            mine = lax.broadcasted_iota(jnp.int32, (2, 1, 1), 0) == upper[step].astype(jnp.int32)
            return jnp.where(mine, value, got).reshape(2 * value.shape[0], value.shape[1])

        def finish(value):
            value = halve(halve(value, 2, jnp.bfloat16), 3, jnp.bfloat16).astype(jnp.bfloat16)
            return double(double(double(value, 3), 2), 1)

        mates = [[i for i in range(cols) if i % 2 == core] for core in range(2)]
        count = cols // 2

        def spread(value):
            return lax.all_to_all(value, "col", 0, 0, tiled=True, axis_index_groups=mates)

        def scatter(value, kind=jnp.float32):
            value = halve(value, 0, jnp.float32)
            parts = spread(value.astype(kind)).astype(jnp.float32)
            return jnp.sum(parts.reshape(count, parts.shape[0] // count, -1), axis=0).astype(jnp.bfloat16)

        def gather(value):
            return spread(jnp.tile(value, (count, 1)))

        def send_row(vectors, shift):
            return lax.ppermute(vectors, "row", [(i, (i + shift) % rows) for i in range(rows)])

        if rows != 2 or len(bits) != 4 or sum(GROUPS) != cholesky.shape[1]:
            rest = jnp.concatenate([send_row(cholesky, shift) for shift in range(1, rows)], axis=1)
            chi = double(gather(scatter(project(amplitudes, cholesky))), 0)
            total = project_back(residual_in, [chi], [cholesky], jnp.float32)
            rest = after(rest, total)
            chi = double(gather(scatter(project(amplitudes, rest))), 0)
            return project_back(total, [chi], [rest], jnp.bfloat16)

        ends = [sum(GROUPS[: k + 1]) for k in range(len(GROUPS))]
        out_a, out_b, out_c = [cholesky[:, end - size : end] for end, size in zip(ends, GROUPS)]
        a = send_row(out_a, 1)
        part_own = project_wide(amplitudes, after(cholesky, out_a))
        keep, send = split(boxed(lambda v: halve(v, 0, jnp.float32), part_own), 1)
        got = exchange(send, bits[1])
        out_b = after(out_b, send)
        b = send_row(out_b, 1)
        part_a = project(amplitudes, after(a, out_b))
        half_own = boxed(finish, after(keep, part_a) + got)
        c = send_row(after(out_c, half_own), 1)
        chi_own = double(half_own, 0)
        part = jnp.concatenate([part_a, project(amplitudes, after(b, chi_own))], axis=1)
        chi_ab = double(boxed(lambda v: gather(scatter(v, jnp.bfloat16)), part), 0)
        chi_c = double(gather(scatter(project(amplitudes, after(c, chi_ab)), jnp.bfloat16)), 0)
        return project_back(residual_in, [chi_own, chi_ab, chi_c], [cholesky, a, b, c], jnp.bfloat16)

    in_specs = (P("row", "col"), P("row", "col"), P("col", "row"))
    return jax.shard_map(body, mesh=mesh, in_specs=in_specs, out_specs=P("row", "col"), check_vma=False)
```

```python
import jax
import jax.numpy as jnp
from jax import lax
from jax.experimental import pallas as pl
from jax.experimental.layout import Layout, with_layout_constraint
from jax.experimental.pallas import tpu as pltpu
from jax.sharding import PartitionSpec as P

GROUPS = (128, 256, 256)
VMEM_BYTES = 58 * 1024 * 1024
FREE = pl.CostEstimate(flops=0, bytes_accessed=0, transcendentals=0)


def after(value, *others):
    return lax.optimization_barrier((value, *others))[0]


def block_of(extent, target):
    while extent % target:
        target //= 2
    return target


def project(amplitudes, vectors):
    part = jnp.dot(amplitudes, vectors, preferred_element_type=jnp.float32)
    return with_layout_constraint(part, Layout(major_to_minor=(0, 1)))


def project_wide(amplitudes, vectors):
    rows, depth = amplitudes.shape
    width = vectors.shape[1]
    block = block_of(depth, 1024)
    steps = depth // block

    def kernel(left_ref, right_ref, out_ref, total_ref):
        step = pl.program_id(0)
        term = lax.dot_general(right_ref[...].T, left_ref[...], (((1,), (1,)), ((), ())), preferred_element_type=jnp.float32)

        @pl.when(step == 0)
        def _():
            total_ref[...] = term

        @pl.when((step > 0) & (step < steps - 1))
        def _():
            total_ref[...] += term

        @pl.when(step == steps - 1)
        def _():
            out_ref[...] = (total_ref[...] + term).T

    return pl.pallas_call(
        kernel,
        grid=(steps,),
        in_specs=[pl.BlockSpec((rows, block), lambda k: (0, k)), pl.BlockSpec((block, width), lambda k: (k, 0))],
        out_specs=pl.BlockSpec((rows, width), lambda k: (0, 0)),
        out_shape=jax.ShapeDtypeStruct((rows, width), jnp.float32),
        scratch_shapes=[pltpu.VMEM((width, rows), jnp.float32)],
        compiler_params=pltpu.CompilerParams(vmem_limit_bytes=VMEM_BYTES),
        cost_estimate=FREE,
    )(amplitudes, vectors)


def project_back(base, chis, pieces, kind):
    rows, columns = base.shape
    block = block_of(columns, 1024)

    def kernel(base_ref, *refs):
        left = jnp.concatenate([c[...] for c in refs[: len(chis)]], axis=1)
        right = jnp.concatenate([p[...] for p in refs[len(chis) : -1]], axis=1)
        term = lax.dot_general(left, right, (((1,), (1,)), ((), ())), preferred_element_type=jnp.float32)
        refs[-1][...] = (base_ref[...].astype(jnp.float32) + term).astype(kind)

    return pl.pallas_call(
        kernel,
        grid=(columns // block,),
        in_specs=[pl.BlockSpec((rows, block), lambda i: (0, i))]
        + [pl.BlockSpec(chi.shape, lambda i: (0, 0), pipeline_mode=pl.Buffered(1)) for chi in chis]
        + [pl.BlockSpec((block, piece.shape[1]), lambda i: (i, 0)) for piece in pieces],
        out_specs=pl.BlockSpec((rows, block), lambda i: (0, i)),
        out_shape=jax.ShapeDtypeStruct(base.shape, kind),
        compiler_params=pltpu.CompilerParams(vmem_limit_bytes=VMEM_BYTES),
        cost_estimate=FREE,
    )(base, *chis, *pieces)


def solution(mesh):
    rows, cols = mesh.shape["row"], mesh.shape["col"]

    def exchange(value, bit):
        return lax.ppermute(value, "col", [(i, i ^ bit) for i in range(cols)])

    def body(amplitudes, residual_in, cholesky):
        me = lax.axis_index("col")
        boxes = (me >> 20) == 0

        def boxed(run, *values):
            def never(*values):
                return jax.tree.map(lambda s: jnp.zeros(s.shape, s.dtype), jax.eval_shape(run, *values))

            return lax.cond(boxes, run, never, *values)

        bits = [1 << k for k in range(cols.bit_length() - 1)]
        upper = [(me & bit) != 0 for bit in bits]

        def split(value, step):
            low, high = jnp.split(value, 2)
            return jnp.where(upper[step], high, low), jnp.where(upper[step], low, high)

        def halve(value, step, kind):
            keep, send = split(value, step)
            return keep + exchange(send.astype(kind), bits[step]).astype(jnp.float32)

        def double(value, step):
            got = exchange(value, bits[step])
            mine = lax.broadcasted_iota(jnp.int32, (2, 1, 1), 0) == upper[step].astype(jnp.int32)
            return jnp.where(mine, value, got).reshape(2 * value.shape[0], value.shape[1])

        def finish(value):
            value = halve(halve(value, 2, jnp.bfloat16), 3, jnp.bfloat16).astype(jnp.bfloat16)
            return double(double(value, 3), 2)

        mates = [[i for i in range(cols) if i % 2 == core] for core in range(2)]
        count = cols // 2

        def spread(value):
            return lax.all_to_all(value, "col", 0, 0, tiled=True, axis_index_groups=mates)

        def chain(value):
            parts = spread(halve(value, 0, jnp.float32).astype(jnp.bfloat16)).astype(jnp.float32)
            mine = jnp.sum(parts.reshape(count, parts.shape[0] // count, -1), axis=0).astype(jnp.bfloat16)
            return spread(jnp.tile(mine, (count, 1)))

        def send_row(vectors, shift):
            return lax.ppermute(vectors, "row", [(i, (i + shift) % rows) for i in range(rows)])

        if rows != 2 or len(bits) != 4 or sum(GROUPS) != cholesky.shape[1]:
            rest = jnp.concatenate([send_row(cholesky, shift) for shift in range(1, rows)], axis=1)
            chi = double(chain(project(amplitudes, cholesky)), 0)
            total = project_back(residual_in, [chi], [cholesky], jnp.float32)
            rest = after(rest, total)
            chi = double(chain(project(amplitudes, rest)), 0)
            return project_back(total, [chi], [rest], jnp.bfloat16)

        ends = [sum(GROUPS[: k + 1]) for k in range(len(GROUPS))]
        out_a, out_b, out_c = [cholesky[:, end - size : end] for end, size in zip(ends, GROUPS)]
        a = send_row(out_a, 1)
        part_own = project_wide(amplitudes, after(cholesky, out_a))
        keep, send = split(boxed(lambda v: halve(v, 0, jnp.float32), part_own), 1)
        got = exchange(send, bits[1])
        out_b = after(out_b, send)
        b = send_row(out_b, 1)
        part_a = project(amplitudes, after(a, out_b))
        quarter = boxed(finish, after(keep, part_a) + got)
        c = send_row(after(out_c, quarter), 1)
        chi_a = double(boxed(chain, after(part_a, quarter)), 0)
        part_b = project(amplitudes, after(b, chi_a))
        chi_own, half_b = boxed(lambda u, v: (double(double(u, 1), 0), chain(v)), quarter, part_b)
        chi_b = double(half_b, 0)
        chi_c = double(chain(project(amplitudes, after(c, chi_b))), 0)
        return project_back(residual_in, [chi_own, chi_a, chi_b, chi_c], [cholesky, a, b, c], jnp.bfloat16)

    in_specs = (P("row", "col"), P("row", "col"), P("col", "row"))
    return jax.shard_map(body, mesh=mesh, in_specs=in_specs, out_specs=P("row", "col"), check_vma=False)
```

```python
import jax
import jax.numpy as jnp
from jax import lax
from jax.experimental import pallas as pl
from jax.experimental.layout import Layout, with_layout_constraint
from jax.experimental.pallas import tpu as pltpu
from jax.sharding import PartitionSpec as P

GROUPS = (128, 256, 256)
VMEM_BYTES = 58 * 1024 * 1024
FREE = pl.CostEstimate(flops=0, bytes_accessed=0, transcendentals=0)


def after(value, *others):
    return lax.optimization_barrier((value, *others))[0]


def block_of(extent, target):
    while extent % target:
        target //= 2
    return target


def project(amplitudes, vectors):
    part = jnp.dot(amplitudes, vectors, preferred_element_type=jnp.float32)
    return with_layout_constraint(part, Layout(major_to_minor=(0, 1)))


def project_wide(amplitudes, vectors):
    rows, depth = amplitudes.shape
    width = vectors.shape[1]
    block = block_of(depth, 1024)
    steps = depth // block

    def kernel(left_ref, right_ref, out_ref, total_ref):
        step = pl.program_id(0)
        term = lax.dot_general(right_ref[...].T, left_ref[...], (((1,), (1,)), ((), ())), preferred_element_type=jnp.float32)

        @pl.when(step == 0)
        def _():
            total_ref[...] = term

        @pl.when((step > 0) & (step < steps - 1))
        def _():
            total_ref[...] += term

        @pl.when(step == steps - 1)
        def _():
            out_ref[...] = (total_ref[...] + term).T

    return pl.pallas_call(
        kernel,
        grid=(steps,),
        in_specs=[pl.BlockSpec((rows, block), lambda k: (0, k)), pl.BlockSpec((block, width), lambda k: (k, 0))],
        out_specs=pl.BlockSpec((rows, width), lambda k: (0, 0)),
        out_shape=jax.ShapeDtypeStruct((rows, width), jnp.float32),
        scratch_shapes=[pltpu.VMEM((width, rows), jnp.float32)],
        compiler_params=pltpu.CompilerParams(vmem_limit_bytes=VMEM_BYTES),
        cost_estimate=FREE,
    )(amplitudes, vectors)


def project_back(base, chis, pieces, upper, kind):
    rows, columns = base.shape
    block = block_of(columns, 1024)
    half = rows // 2
    widths = [mine.shape[1] for mine, _ in chis]

    def kernel(upper_ref, base_ref, *refs):
        chi_refs, piece_refs, (out_ref, left_ref) = refs[: 2 * len(chis)], refs[2 * len(chis) : -2], refs[-2:]

        @pl.when(pl.program_id(0) == 0)
        def _():
            own = pl.multiple_of(upper_ref[0] * half, half)
            other = pl.multiple_of((1 - upper_ref[0]) * half, half)
            at = 0
            for k, width in enumerate(widths):
                left_ref[pl.ds(own, half), at : at + width] = chi_refs[2 * k][...]
                left_ref[pl.ds(other, half), at : at + width] = chi_refs[2 * k + 1][...]
                at += width

        right = jnp.concatenate([p[...] for p in piece_refs], axis=1)
        term = lax.dot_general(left_ref[...], right, (((1,), (1,)), ((), ())), preferred_element_type=jnp.float32)
        out_ref[...] = (base_ref[...].astype(jnp.float32) + term).astype(kind)

    halves = [h for pair in chis for h in pair]
    return pl.pallas_call(
        kernel,
        grid_spec=pltpu.PrefetchScalarGridSpec(
            num_scalar_prefetch=1,
            grid=(columns // block,),
            in_specs=[pl.BlockSpec((rows, block), lambda i, u: (0, i))]
            + [pl.BlockSpec(h.shape, lambda i, u: (0, 0), pipeline_mode=pl.Buffered(1)) for h in halves]
            + [pl.BlockSpec((block, piece.shape[1]), lambda i, u: (i, 0)) for piece in pieces],
            out_specs=pl.BlockSpec((rows, block), lambda i, u: (0, i)),
            scratch_shapes=[pltpu.VMEM((rows, sum(widths)), jnp.bfloat16)],
        ),
        out_shape=jax.ShapeDtypeStruct(base.shape, kind),
        compiler_params=pltpu.CompilerParams(vmem_limit_bytes=VMEM_BYTES),
        cost_estimate=FREE,
    )(upper, base, *halves, *pieces)


def solution(mesh):
    rows, cols = mesh.shape["row"], mesh.shape["col"]

    def exchange(value, bit):
        return lax.ppermute(value, "col", [(i, i ^ bit) for i in range(cols)])

    def body(amplitudes, residual_in, cholesky):
        me = lax.axis_index("col")
        boxes = (me >> 20) == 0

        def boxed(run, *values):
            def never(*values):
                return jax.tree.map(lambda s: jnp.zeros(s.shape, s.dtype), jax.eval_shape(run, *values))

            return lax.cond(boxes, run, never, *values)

        bits = [1 << k for k in range(cols.bit_length() - 1)]
        upper = [(me & bit) != 0 for bit in bits]

        def split(value, step):
            low, high = jnp.split(value, 2)
            return jnp.where(upper[step], high, low), jnp.where(upper[step], low, high)

        def halve(value, step, kind):
            keep, send = split(value, step)
            return keep + exchange(send.astype(kind), bits[step]).astype(jnp.float32)

        def double(value, step):
            got = exchange(value, bits[step])
            mine = lax.broadcasted_iota(jnp.int32, (2, 1, 1), 0) == upper[step].astype(jnp.int32)
            return jnp.where(mine, value, got).reshape(2 * value.shape[0], value.shape[1])

        def finish(value):
            value = halve(halve(value, 2, jnp.bfloat16), 3, jnp.bfloat16).astype(jnp.bfloat16)
            return double(double(value, 3), 2)

        def both(value):
            return value, exchange(value, 1)

        flag = jnp.reshape(me & 1, (1,))
        mates = [[i for i in range(cols) if i % 2 == core] for core in range(2)]
        count = cols // 2

        def spread(value):
            return lax.all_to_all(value, "col", 0, 0, tiled=True, axis_index_groups=mates)

        def scatter(value):
            parts = spread(halve(value, 0, jnp.float32).astype(jnp.bfloat16)).astype(jnp.float32)
            return jnp.sum(parts.reshape(count, parts.shape[0] // count, -1), axis=0).astype(jnp.bfloat16)

        def gather(mine):
            return spread(jnp.tile(mine, (count, 1)))

        def chain(value):
            return gather(scatter(value))

        def last(quarter, part):
            mine = scatter(part)
            return both(after(double(quarter, 1), mine)), gather(mine)

        def send_row(vectors, shift):
            return lax.ppermute(vectors, "row", [(i, (i + shift) % rows) for i in range(rows)])

        if rows != 2 or len(bits) != 4 or sum(GROUPS) != cholesky.shape[1]:
            rest = jnp.concatenate([send_row(cholesky, shift) for shift in range(1, rows)], axis=1)
            pair = both(chain(project(amplitudes, cholesky)))
            total = project_back(residual_in, [pair], [cholesky], flag, jnp.float32)
            rest = after(rest, total)
            pair = both(chain(project(amplitudes, rest)))
            return project_back(total, [pair], [rest], flag, jnp.bfloat16)

        ends = [sum(GROUPS[: k + 1]) for k in range(len(GROUPS))]
        out_a, out_b, out_c = [cholesky[:, end - size : end] for end, size in zip(ends, GROUPS)]
        a = send_row(out_a, 1)
        part_own = project_wide(amplitudes, after(cholesky, out_a))
        keep, send = split(boxed(lambda v: halve(v, 0, jnp.float32), part_own), 1)
        got = exchange(send, bits[1])
        out_b = after(out_b, send)
        b = send_row(out_b, 1)
        part_a = project(amplitudes, after(a, out_b))
        quarter = boxed(finish, after(keep, part_a) + got)
        c = send_row(after(out_c, quarter), 1)
        part = jnp.concatenate([part_a, project(amplitudes, after(b, quarter))], axis=1)
        own, half_ab = boxed(last, quarter, part)
        pair_ab = both(half_ab)
        pair_c = both(chain(project(amplitudes, after(c, *pair_ab))))
        return project_back(residual_in, [own, pair_ab, pair_c], [cholesky, a, b, c], flag, jnp.bfloat16)

    in_specs = (P("row", "col"), P("row", "col"), P("col", "row"))
    return jax.shard_map(body, mesh=mesh, in_specs=in_specs, out_specs=P("row", "col"), check_vma=False)
```

```python
import functools

import jax
import jax.numpy as jnp
from jax import lax
from jax.experimental import pallas as pl
from jax.experimental.layout import Layout, with_layout_constraint
from jax.experimental.pallas import tpu as pltpu
from jax.sharding import PartitionSpec as P

GROUPS = (128, 256, 256)
VMEM_BYTES = 58 * 1024 * 1024
FREE = pl.CostEstimate(flops=0, bytes_accessed=0, transcendentals=0)


def after(value, *others):
    return lax.optimization_barrier((value, *others))[0]


def block_of(extent, target):
    while extent % target:
        target //= 2
    return target


def project(amplitudes, vectors):
    part = jnp.dot(amplitudes, vectors, preferred_element_type=jnp.float32)
    return with_layout_constraint(part, Layout(major_to_minor=(0, 1)))


def project_wide(amplitudes, vectors):
    rows, depth = amplitudes.shape
    width = vectors.shape[1]
    block = block_of(depth, 1024)
    steps = depth // block

    def kernel(left_ref, right_ref, out_ref, total_ref):
        step = pl.program_id(0)
        term = lax.dot_general(right_ref[...].T, left_ref[...], (((1,), (1,)), ((), ())), preferred_element_type=jnp.float32)

        @pl.when(step == 0)
        def _():
            total_ref[...] = term

        @pl.when((step > 0) & (step < steps - 1))
        def _():
            total_ref[...] += term

        @pl.when(step == steps - 1)
        def _():
            out_ref[...] = (total_ref[...] + term).T

    return pl.pallas_call(
        kernel,
        grid=(steps,),
        in_specs=[pl.BlockSpec((rows, block), lambda k: (0, k)), pl.BlockSpec((block, width), lambda k: (k, 0))],
        out_specs=pl.BlockSpec((rows, width), lambda k: (0, 0)),
        out_shape=jax.ShapeDtypeStruct((rows, width), jnp.float32),
        scratch_shapes=[pltpu.VMEM((width, rows), jnp.float32)],
        compiler_params=pltpu.CompilerParams(vmem_limit_bytes=VMEM_BYTES),
        cost_estimate=FREE,
    )(amplitudes, vectors)


def project_back(base, chis, pieces, upper, kind, share=(0, 1), earlier=None):
    rows, columns = base.shape
    block = block_of(columns // share[1], 1024)
    steps = columns // share[1] // block
    first = share[0] * steps
    half = rows // 2
    widths = [mine.shape[1] for mine, _ in chis]

    def kernel(upper_ref, base_ref, *refs):
        refs = refs if earlier is None else refs[1:]
        chi_refs, piece_refs, (out_ref, left_ref) = refs[: 2 * len(chis)], refs[2 * len(chis) : -2], refs[-2:]

        @pl.when(pl.program_id(0) == 0)
        def _():
            own = pl.multiple_of(upper_ref[0] * half, half)
            other = pl.multiple_of((1 - upper_ref[0]) * half, half)
            at = 0
            for k, width in enumerate(widths):
                left_ref[pl.ds(own, half), at : at + width] = chi_refs[2 * k][...]
                left_ref[pl.ds(other, half), at : at + width] = chi_refs[2 * k + 1][...]
                at += width

        right = jnp.concatenate([p[...] for p in piece_refs], axis=1)
        term = lax.dot_general(left_ref[...], right, (((1,), (1,)), ((), ())), preferred_element_type=jnp.float32)
        out_ref[...] = (base_ref[...].astype(jnp.float32) + term).astype(kind)

    halves = [h for pair in chis for h in pair]
    return pl.pallas_call(
        kernel,
        grid_spec=pltpu.PrefetchScalarGridSpec(
            num_scalar_prefetch=1,
            grid=(steps,),
            in_specs=[pl.BlockSpec((rows, block), lambda i, u: (0, i + first))]
            + ([] if earlier is None else [pl.BlockSpec(memory_space=pl.ANY)])
            + [pl.BlockSpec(h.shape, lambda i, u: (0, 0), pipeline_mode=pl.Buffered(1)) for h in halves]
            + [pl.BlockSpec((block, piece.shape[1]), lambda i, u: (i + first, 0)) for piece in pieces],
            out_specs=pl.BlockSpec((rows, block), lambda i, u: (0, i + first)),
            scratch_shapes=[pltpu.VMEM((rows, sum(widths)), jnp.bfloat16)],
        ),
        out_shape=jax.ShapeDtypeStruct(base.shape, kind),
        input_output_aliases={} if earlier is None else {2: 0},
        compiler_params=pltpu.CompilerParams(vmem_limit_bytes=VMEM_BYTES),
        cost_estimate=pl.CostEstimate(
            flops=2 * rows * steps * block * sum(widths),
            bytes_accessed=rows * steps * block * (base.dtype.itemsize + jnp.dtype(kind).itemsize),
            transcendentals=0,
        ),
    )(upper, base, *([] if earlier is None else [earlier]), *halves, *pieces)


def solution(mesh):
    rows, cols = mesh.shape["row"], mesh.shape["col"]

    def exchange(value, bit):
        return lax.ppermute(value, "col", [(i, i ^ bit) for i in range(cols)])

    def body(amplitudes, residual_in, cholesky):
        me = lax.axis_index("col")
        boxes = (me >> 20) == 0

        def boxed(run, *values):
            def never(*values):
                return jax.tree.map(lambda s: jnp.zeros(s.shape, s.dtype), jax.eval_shape(run, *values))

            return lax.cond(boxes, run, never, *values)

        bits = [1 << k for k in range(cols.bit_length() - 1)]
        upper = [(me & bit) != 0 for bit in bits]

        def split(value, step):
            low, high = jnp.split(value, 2)
            return jnp.where(upper[step], high, low), jnp.where(upper[step], low, high)

        def halve(value, step, kind):
            keep, send = split(value, step)
            return keep + exchange(send.astype(kind), bits[step]).astype(jnp.float32)

        def double(value, step):
            got = exchange(value, bits[step])
            mine = lax.broadcasted_iota(jnp.int32, (2, 1, 1), 0) == upper[step].astype(jnp.int32)
            return jnp.where(mine, value, got).reshape(2 * value.shape[0], value.shape[1])

        def finish(value):
            value = halve(halve(value, 2, jnp.float32), 3, jnp.float32).astype(jnp.bfloat16)
            return double(double(value, 3), 2)

        def both(value):
            return value, exchange(value, 1)

        flag = jnp.reshape(me & 1, (1,))
        mates = [[i for i in range(cols) if i % 2 == core] for core in range(2)]
        count = cols // 2

        def spread(value):
            return lax.all_to_all(value, "col", 0, 0, tiled=True, axis_index_groups=mates)

        def scatter(value):
            parts = spread(halve(value, 0, jnp.float32).astype(jnp.bfloat16)).astype(jnp.float32)
            return jnp.sum(parts.reshape(count, parts.shape[0] // count, -1), axis=0).astype(jnp.bfloat16)

        def gather(mine):
            return spread(jnp.tile(mine, (count, 1)))

        def chain(value):
            return gather(scatter(value))

        def last(quarter, part):
            mine = scatter(part)
            return both(after(double(quarter, 1), mine)), gather(mine)

        def send_row(vectors, shift):
            return lax.ppermute(vectors, "row", [(i, (i + shift) % rows) for i in range(rows)])

        if rows != 2 or len(bits) != 4 or sum(GROUPS) != cholesky.shape[1]:
            rest = jnp.concatenate([send_row(cholesky, shift) for shift in range(1, rows)], axis=1)
            pair = both(chain(project(amplitudes, cholesky)))
            total = project_back(residual_in, [pair], [cholesky], flag, jnp.float32)
            rest = after(rest, total)
            pair = both(chain(project(amplitudes, rest)))
            return project_back(total, [pair], [rest], flag, jnp.bfloat16)

        ends = [sum(GROUPS[: k + 1]) for k in range(len(GROUPS))]
        out_a, out_b, out_c = [cholesky[:, end - size : end] for end, size in zip(ends, GROUPS)]
        a = send_row(out_a, 1)
        part_own = project_wide(amplitudes, after(cholesky, out_a))
        keep, send = split(boxed(lambda v: halve(v, 0, jnp.float32), part_own), 1)
        got = exchange(send, bits[1])
        out_b = after(out_b, send)
        b = send_row(out_b, 1)
        part_a = project(amplitudes, after(a, out_b))
        quarter = boxed(finish, after(keep, part_a) + got)
        c = send_row(after(out_c, quarter), 1)
        part = jnp.concatenate([part_a, project(amplitudes, after(b, quarter))], axis=1)
        own, half_ab = boxed(last, quarter, part)
        pair_ab = both(half_ab)
        part_c = project(amplitudes, after(c, *pair_ab))

        def tail(part, residual, own, pair, *pieces):
            done = functools.partial(project_back, chis=[own, pair], pieces=pieces, upper=flag, kind=jnp.float32)
            total = done(residual, share=(0, 2))
            mine = after(scatter(part), total)
            total = done(after(residual, mine), share=(1, 2), earlier=total)
            return after(gather(mine), total), total

        half_c, total = boxed(tail, part_c, residual_in, own, pair_ab, cholesky, a, b)
        return project_back(total, [both(half_c)], [c], flag, jnp.bfloat16)

    in_specs = (P("row", "col"), P("row", "col"), P("col", "row"))
    return jax.shard_map(body, mesh=mesh, in_specs=in_specs, out_specs=P("row", "col"), check_vma=False)
```

```python
import jax
import jax.numpy as jnp
from jax import lax
from jax.experimental import pallas as pl
from jax.experimental.pallas import tpu as pltpu
from jax.sharding import PartitionSpec as P

GROUPS = (128, 256, 256)
VMEM_BYTES = 58 * 1024 * 1024
FREE = pl.CostEstimate(flops=0, bytes_accessed=0, transcendentals=0)


def after(value, *others):
    return lax.optimization_barrier((value, *others))[0]


def block_of(extent, target):
    while extent % target:
        target //= 2
    return target


def project(amplitudes, vectors):
    rows, depth = amplitudes.shape
    width = vectors.shape[1]
    block = block_of(depth, 512)
    part = block_of(rows, 256)

    def kernel(left_ref, right_ref, out_ref):
        for at in range(0, rows, part):
            cut = slice(at, at + part)
            term = jnp.dot(left_ref[cut, :], right_ref[...], preferred_element_type=jnp.float32)

            @pl.when(pl.program_id(0) == 0)
            def _():
                out_ref[cut, :] = term

            @pl.when(pl.program_id(0) > 0)
            def _():
                out_ref[cut, :] += term

    return pl.pallas_call(
        kernel,
        grid=(depth // block,),
        in_specs=[pl.BlockSpec((rows, block), lambda k: (0, k)), pl.BlockSpec((block, width), lambda k: (k, 0))],
        out_specs=pl.BlockSpec((rows, width), lambda k: (0, 0)),
        out_shape=jax.ShapeDtypeStruct((rows, width), jnp.float32),
        compiler_params=pltpu.CompilerParams(vmem_limit_bytes=VMEM_BYTES),
        cost_estimate=FREE,
    )(amplitudes, vectors)


def project_wide(amplitudes, vectors):
    rows, depth = amplitudes.shape
    width = vectors.shape[1]
    block = block_of(depth, 1024)
    steps = depth // block

    def kernel(left_ref, right_ref, out_ref, total_ref):
        step = pl.program_id(0)
        term = lax.dot_general(right_ref[...].T, left_ref[...], (((1,), (1,)), ((), ())), preferred_element_type=jnp.float32)

        @pl.when(step == 0)
        def _():
            total_ref[...] = term

        @pl.when((step > 0) & (step < steps - 1))
        def _():
            total_ref[...] += term

        @pl.when(step == steps - 1)
        def _():
            out_ref[...] = (total_ref[...] + term).T

    return pl.pallas_call(
        kernel,
        grid=(steps,),
        in_specs=[pl.BlockSpec((rows, block), lambda k: (0, k)), pl.BlockSpec((block, width), lambda k: (k, 0))],
        out_specs=pl.BlockSpec((rows, width), lambda k: (0, 0)),
        out_shape=jax.ShapeDtypeStruct((rows, width), jnp.float32),
        scratch_shapes=[pltpu.VMEM((width, rows), jnp.float32)],
        compiler_params=pltpu.CompilerParams(vmem_limit_bytes=VMEM_BYTES),
        cost_estimate=FREE,
    )(amplitudes, vectors)


def project_back(base, chis, pieces, upper, kind):
    rows, columns = base.shape
    block = block_of(columns, 1024)
    half = rows // 2
    widths = [mine.shape[1] for mine, _ in chis]

    def kernel(upper_ref, base_ref, *refs):
        chi_refs, piece_refs, (out_ref, left_ref) = refs[: 2 * len(chis)], refs[2 * len(chis) : -2], refs[-2:]

        @pl.when(pl.program_id(0) == 0)
        def _():
            own = pl.multiple_of(upper_ref[0] * half, half)
            other = pl.multiple_of((1 - upper_ref[0]) * half, half)
            at = 0
            for k, width in enumerate(widths):
                left_ref[pl.ds(own, half), at : at + width] = chi_refs[2 * k][...]
                left_ref[pl.ds(other, half), at : at + width] = chi_refs[2 * k + 1][...]
                at += width

        right = jnp.concatenate([p[...] for p in piece_refs], axis=1)
        term = lax.dot_general(left_ref[...], right, (((1,), (1,)), ((), ())), preferred_element_type=jnp.float32)
        out_ref[...] = (base_ref[...].astype(jnp.float32) + term).astype(kind)

    halves = [h for pair in chis for h in pair]
    return pl.pallas_call(
        kernel,
        grid_spec=pltpu.PrefetchScalarGridSpec(
            num_scalar_prefetch=1,
            grid=(columns // block,),
            in_specs=[pl.BlockSpec((rows, block), lambda i, u: (0, i))]
            + [pl.BlockSpec(h.shape, lambda i, u: (0, 0), pipeline_mode=pl.Buffered(1)) for h in halves]
            + [pl.BlockSpec((block, piece.shape[1]), lambda i, u: (i, 0)) for piece in pieces],
            out_specs=pl.BlockSpec((rows, block), lambda i, u: (0, i)),
            scratch_shapes=[pltpu.VMEM((rows, sum(widths)), jnp.bfloat16)],
        ),
        out_shape=jax.ShapeDtypeStruct(base.shape, kind),
        compiler_params=pltpu.CompilerParams(vmem_limit_bytes=VMEM_BYTES),
        cost_estimate=FREE,
    )(upper, base, *halves, *pieces)


def solution(mesh):
    rows, cols = mesh.shape["row"], mesh.shape["col"]

    def exchange(value, bit):
        return lax.ppermute(value, "col", [(i, i ^ bit) for i in range(cols)])

    def body(amplitudes, residual_in, cholesky):
        me = lax.axis_index("col")
        boxes = (me >> 20) == 0

        def boxed(run, *values):
            def never(*values):
                return jax.tree.map(lambda s: jnp.zeros(s.shape, s.dtype), jax.eval_shape(run, *values))

            return lax.cond(boxes, run, never, *values)

        bits = [1 << k for k in range(cols.bit_length() - 1)]
        upper = [(me & bit) != 0 for bit in bits]

        def split(value, step):
            low, high = jnp.split(value, 2)
            return jnp.where(upper[step], high, low), jnp.where(upper[step], low, high)

        def halve(value, step, kind):
            keep, send = split(value, step)
            return keep + exchange(send.astype(kind), bits[step]).astype(jnp.float32)

        def double(value, step):
            got = exchange(value, bits[step])
            mine = lax.broadcasted_iota(jnp.int32, (2, 1, 1), 0) == upper[step].astype(jnp.int32)
            return jnp.where(mine, value, got).reshape(2 * value.shape[0], value.shape[1])

        def finish(value):
            value = halve(halve(value, 2, jnp.float32), 3, jnp.float32).astype(jnp.bfloat16)
            return double(double(value, 3), 2)

        def both(value):
            return value, exchange(value, 1)

        flag = jnp.reshape(me & 1, (1,))
        mates = [[i for i in range(cols) if i % 2 == core] for core in range(2)]
        count = cols // 2

        def spread(value):
            return lax.all_to_all(value, "col", 0, 0, tiled=True, axis_index_groups=mates)

        def scatter(value):
            parts = spread(halve(value, 0, jnp.float32).astype(jnp.bfloat16)).astype(jnp.float32)
            return jnp.sum(parts.reshape(count, parts.shape[0] // count, -1), axis=0).astype(jnp.bfloat16)

        def gather(mine):
            return spread(jnp.tile(mine, (count, 1)))

        def chain(value):
            return gather(scatter(value))

        def last(quarter, part):
            mine = scatter(part)
            return both(after(double(quarter, 1), mine)), gather(mine)

        def send_row(vectors, shift):
            return lax.ppermute(vectors, "row", [(i, (i + shift) % rows) for i in range(rows)])

        if rows != 2 or len(bits) != 4 or sum(GROUPS) != cholesky.shape[1]:
            rest = jnp.concatenate([send_row(cholesky, shift) for shift in range(1, rows)], axis=1)
            pair = both(chain(project(amplitudes, cholesky)))
            total = project_back(residual_in, [pair], [cholesky], flag, jnp.float32)
            rest = after(rest, total)
            pair = both(chain(project(amplitudes, rest)))
            return project_back(total, [pair], [rest], flag, jnp.bfloat16)

        ends = [sum(GROUPS[: k + 1]) for k in range(len(GROUPS))]
        out_a, out_b, out_c = [cholesky[:, end - size : end] for end, size in zip(ends, GROUPS)]
        a = send_row(out_a, 1)
        part_own = project_wide(amplitudes, after(cholesky, out_a))
        keep, send = split(boxed(lambda v: halve(v, 0, jnp.float32), part_own), 1)
        got = exchange(send, bits[1])
        out_b = after(out_b, send)
        b = send_row(out_b, 1)
        part_a = project(amplitudes, after(a, out_b))
        quarter = boxed(finish, after(keep, part_a) + got)
        c = send_row(after(out_c, quarter), 1)
        part = jnp.concatenate([part_a, project(amplitudes, after(b, quarter))], axis=1)
        own, half_ab = boxed(last, quarter, part)
        pair_ab = both(half_ab)
        pair_c = both(chain(project(amplitudes, after(c, *pair_ab))))
        return project_back(residual_in, [own, pair_ab, pair_c], [cholesky, a, b, c], flag, jnp.bfloat16)

    in_specs = (P("row", "col"), P("row", "col"), P("col", "row"))
    return jax.shard_map(body, mesh=mesh, in_specs=in_specs, out_specs=P("row", "col"), check_vma=False)
```

```python
import functools

import jax
import jax.numpy as jnp
from jax import lax
from jax.experimental import pallas as pl
from jax.experimental.layout import Layout, with_layout_constraint
from jax.experimental.pallas import tpu as pltpu
from jax.sharding import PartitionSpec as P

GROUPS = (128, 256, 256)
VMEM_BYTES = 58 * 1024 * 1024
TAIL_VMEM_BYTES = 34 * 1024 * 1024
FREE = pl.CostEstimate(flops=0, bytes_accessed=0, transcendentals=0)


def after(value, *others):
    return lax.optimization_barrier((value, *others))[0]


def block_of(extent, target):
    while extent % target:
        target //= 2
    return target


def project(amplitudes, vectors):
    part = jnp.dot(amplitudes, vectors, preferred_element_type=jnp.float32)
    return with_layout_constraint(part, Layout(major_to_minor=(0, 1)))


def project_wide(amplitudes, vectors):
    rows, depth = amplitudes.shape
    width = vectors.shape[1]
    block = block_of(depth, 1024)
    steps = depth // block

    def kernel(left_ref, right_ref, out_ref, total_ref):
        step = pl.program_id(0)
        term = lax.dot_general(right_ref[...].T, left_ref[...], (((1,), (1,)), ((), ())), preferred_element_type=jnp.float32)

        @pl.when(step == 0)
        def _():
            total_ref[...] = term

        @pl.when((step > 0) & (step < steps - 1))
        def _():
            total_ref[...] += term

        @pl.when(step == steps - 1)
        def _():
            out_ref[...] = (total_ref[...] + term).T

    return pl.pallas_call(
        kernel,
        grid=(steps,),
        in_specs=[pl.BlockSpec((rows, block), lambda k: (0, k)), pl.BlockSpec((block, width), lambda k: (k, 0))],
        out_specs=pl.BlockSpec((rows, width), lambda k: (0, 0)),
        out_shape=jax.ShapeDtypeStruct((rows, width), jnp.float32),
        scratch_shapes=[pltpu.VMEM((width, rows), jnp.float32)],
        compiler_params=pltpu.CompilerParams(vmem_limit_bytes=VMEM_BYTES),
        cost_estimate=FREE,
    )(amplitudes, vectors)


def project_back(base, chis, pieces, upper, kind, share=(0, 1), earlier=None):
    rows, columns = base.shape
    block = block_of(columns // share[1], 1024)
    steps = columns // share[1] // block
    first = share[0] * steps
    half = rows // 2
    widths = [mine.shape[1] for mine, _ in chis]

    def kernel(upper_ref, base_ref, *refs):
        refs = refs if earlier is None else refs[1:]
        chi_refs, piece_refs, (out_ref, left_ref) = refs[: 2 * len(chis)], refs[2 * len(chis) : -2], refs[-2:]

        @pl.when(pl.program_id(0) == 0)
        def _():
            own = pl.multiple_of(upper_ref[0] * half, half)
            other = pl.multiple_of((1 - upper_ref[0]) * half, half)
            at = 0
            for k, width in enumerate(widths):
                left_ref[pl.ds(own, half), at : at + width] = chi_refs[2 * k][...]
                left_ref[pl.ds(other, half), at : at + width] = chi_refs[2 * k + 1][...]
                at += width

        right = jnp.concatenate([p[...] for p in piece_refs], axis=1)
        term = lax.dot_general(left_ref[...], right, (((1,), (1,)), ((), ())), preferred_element_type=jnp.float32)
        out_ref[...] = (base_ref[...].astype(jnp.float32) + term).astype(kind)

    halves = [h for pair in chis for h in pair]
    return pl.pallas_call(
        kernel,
        grid_spec=pltpu.PrefetchScalarGridSpec(
            num_scalar_prefetch=1,
            grid=(steps,),
            in_specs=[pl.BlockSpec((rows, block), lambda i, u: (0, i + first))]
            + ([] if earlier is None else [pl.BlockSpec(memory_space=pl.ANY)])
            + [pl.BlockSpec(h.shape, lambda i, u: (0, 0), pipeline_mode=pl.Buffered(1)) for h in halves]
            + [pl.BlockSpec((block, piece.shape[1]), lambda i, u: (i + first, 0)) for piece in pieces],
            out_specs=pl.BlockSpec((rows, block), lambda i, u: (0, i + first)),
            scratch_shapes=[pltpu.VMEM((rows, sum(widths)), jnp.bfloat16)],
        ),
        out_shape=jax.ShapeDtypeStruct(base.shape, kind),
        input_output_aliases={} if earlier is None else {2: 0},
        compiler_params=pltpu.CompilerParams(vmem_limit_bytes=TAIL_VMEM_BYTES),
        cost_estimate=pl.CostEstimate(
            flops=2 * rows * steps * block * sum(widths),
            bytes_accessed=rows * steps * block * (base.dtype.itemsize + jnp.dtype(kind).itemsize),
            transcendentals=0,
        ),
    )(upper, base, *([] if earlier is None else [earlier]), *halves, *pieces)


def solution(mesh):
    rows, cols = mesh.shape["row"], mesh.shape["col"]

    def exchange(value, bit):
        return lax.ppermute(value, "col", [(i, i ^ bit) for i in range(cols)])

    def body(amplitudes, residual_in, cholesky):
        me = lax.axis_index("col")
        boxes = (me >> 20) == 0

        def boxed(run, *values):
            def never(*values):
                return jax.tree.map(lambda s: jnp.zeros(s.shape, s.dtype), jax.eval_shape(run, *values))

            return lax.cond(boxes, run, never, *values)

        bits = [1 << k for k in range(cols.bit_length() - 1)]
        upper = [(me & bit) != 0 for bit in bits]

        def split(value, step):
            low, high = jnp.split(value, 2)
            return jnp.where(upper[step], high, low), jnp.where(upper[step], low, high)

        def halve(value, step, kind):
            keep, send = split(value, step)
            return keep + exchange(send.astype(kind), bits[step]).astype(jnp.float32)

        def double(value, step):
            got = exchange(value, bits[step])
            mine = lax.broadcasted_iota(jnp.int32, (2, 1, 1), 0) == upper[step].astype(jnp.int32)
            return jnp.where(mine, value, got).reshape(2 * value.shape[0], value.shape[1])

        def finish(value):
            value = halve(halve(value, 2, jnp.float32), 3, jnp.float32).astype(jnp.bfloat16)
            return double(double(value, 3), 2)

        def both(value):
            return value, exchange(value, 1)

        flag = jnp.reshape(me & 1, (1,))
        mates = [[i for i in range(cols) if i % 2 == core] for core in range(2)]
        count = cols // 2

        def spread(value):
            return lax.all_to_all(value, "col", 0, 0, tiled=True, axis_index_groups=mates)

        def scatter(value):
            parts = spread(halve(value, 0, jnp.float32).astype(jnp.bfloat16)).astype(jnp.float32)
            return jnp.sum(parts.reshape(count, parts.shape[0] // count, -1), axis=0).astype(jnp.bfloat16)

        def gather(mine):
            return spread(jnp.tile(mine, (count, 1)))

        def chain(value):
            return gather(scatter(value))

        def last(quarter, part):
            mine = scatter(part)
            return both(after(double(quarter, 1), mine)), gather(mine)

        def send_row(vectors, shift):
            return lax.ppermute(vectors, "row", [(i, (i + shift) % rows) for i in range(rows)])

        if rows != 2 or len(bits) != 4 or sum(GROUPS) != cholesky.shape[1]:
            rest = jnp.concatenate([send_row(cholesky, shift) for shift in range(1, rows)], axis=1)
            pair = both(chain(project(amplitudes, cholesky)))
            total = project_back(residual_in, [pair], [cholesky], flag, jnp.float32)
            rest = after(rest, total)
            pair = both(chain(project(amplitudes, rest)))
            return project_back(total, [pair], [rest], flag, jnp.bfloat16)

        ends = [sum(GROUPS[: k + 1]) for k in range(len(GROUPS))]
        out_a, out_b, out_c = [cholesky[:, end - size : end] for end, size in zip(ends, GROUPS)]
        a = send_row(out_a, 1)
        part_own = project_wide(amplitudes, after(cholesky, out_a))
        keep, send = split(boxed(lambda v: halve(v, 0, jnp.float32), part_own), 1)
        got = exchange(send, bits[1])
        out_b = after(out_b, send)
        b = send_row(out_b, 1)
        part_a = project(amplitudes, after(a, out_b))
        quarter = boxed(finish, after(keep, part_a) + got)
        c = send_row(after(out_c, quarter), 1)
        part = jnp.concatenate([part_a, project(amplitudes, after(b, quarter))], axis=1)
        own, half_ab = boxed(last, quarter, part)
        pair_ab = both(half_ab)
        part_c = project(amplitudes, after(c, *pair_ab))

        def tail(part, residual, own, pair, *pieces):
            done = functools.partial(project_back, chis=[own, pair], pieces=pieces, upper=flag, kind=jnp.float32)
            total = done(residual, share=(0, 2))
            mine = after(scatter(part), total)
            total = done(after(residual, mine), share=(1, 2), earlier=total)
            pair_c = both(after(gather(mine), total))
            return project_back(total, [pair_c], [c], flag, jnp.bfloat16)

        return boxed(tail, part_c, residual_in, own, pair_ab, cholesky, a, b)

    in_specs = (P("row", "col"), P("row", "col"), P("col", "row"))
    return jax.shard_map(body, mesh=mesh, in_specs=in_specs, out_specs=P("row", "col"), check_vma=False)
```

```python
import functools

import jax
import jax.numpy as jnp
from jax import lax
from jax.experimental import pallas as pl
from jax.experimental.layout import Layout, with_layout_constraint
from jax.experimental.pallas import tpu as pltpu
from jax.sharding import PartitionSpec as P

GROUPS = (128, 256, 256)
VMEM_BYTES = 50 * 1024 * 1024
FREE = pl.CostEstimate(flops=0, bytes_accessed=0, transcendentals=0)


def after(value, *others):
    return lax.optimization_barrier((value, *others))[0]


def block_of(extent, target):
    while extent % target:
        target //= 2
    return target


def project(amplitudes, vectors):
    part = jnp.dot(amplitudes, vectors, preferred_element_type=jnp.float32)
    return with_layout_constraint(part, Layout(major_to_minor=(0, 1)))


def project_wide(amplitudes, vectors):
    rows, depth = amplitudes.shape
    width = vectors.shape[1]
    block = block_of(depth, 1024)
    steps = depth // block

    def kernel(left_ref, right_ref, out_ref, total_ref):
        step = pl.program_id(0)
        term = lax.dot_general(right_ref[...].T, left_ref[...], (((1,), (1,)), ((), ())), preferred_element_type=jnp.float32)

        @pl.when(step == 0)
        def _():
            total_ref[...] = term

        @pl.when((step > 0) & (step < steps - 1))
        def _():
            total_ref[...] += term

        @pl.when(step == steps - 1)
        def _():
            out_ref[...] = (total_ref[...] + term).T

    return pl.pallas_call(
        kernel,
        grid=(steps,),
        in_specs=[pl.BlockSpec((rows, block), lambda k: (0, k)), pl.BlockSpec((block, width), lambda k: (k, 0))],
        out_specs=pl.BlockSpec((rows, width), lambda k: (0, 0)),
        out_shape=jax.ShapeDtypeStruct((rows, width), jnp.float32),
        scratch_shapes=[pltpu.VMEM((width, rows), jnp.float32)],
        compiler_params=pltpu.CompilerParams(vmem_limit_bytes=VMEM_BYTES),
        cost_estimate=FREE,
    )(amplitudes, vectors)


def project_back(base, chis, pieces, upper, kind, share=(0, 1), earlier=None):
    rows, columns = base.shape
    block = block_of(columns // share[1], 1024)
    steps = columns // share[1] // block
    first = share[0] * steps
    half = rows // 2
    widths = [mine.shape[1] for mine, _ in chis]

    def kernel(upper_ref, base_ref, *refs):
        refs = refs if earlier is None else refs[1:]
        chi_refs, piece_refs, (out_ref, left_ref) = refs[: 2 * len(chis)], refs[2 * len(chis) : -2], refs[-2:]

        @pl.when(pl.program_id(0) == 0)
        def _():
            own = pl.multiple_of(upper_ref[0] * half, half)
            other = pl.multiple_of((1 - upper_ref[0]) * half, half)
            at = 0
            for k, width in enumerate(widths):
                left_ref[pl.ds(own, half), at : at + width] = chi_refs[2 * k][...]
                left_ref[pl.ds(other, half), at : at + width] = chi_refs[2 * k + 1][...]
                at += width

        right = jnp.concatenate([p[...] for p in piece_refs], axis=1)
        term = lax.dot_general(left_ref[...], right, (((1,), (1,)), ((), ())), preferred_element_type=jnp.float32)
        out_ref[...] = (base_ref[...].astype(jnp.float32) + term).astype(kind)

    halves = [h for pair in chis for h in pair]
    return pl.pallas_call(
        kernel,
        grid_spec=pltpu.PrefetchScalarGridSpec(
            num_scalar_prefetch=1,
            grid=(steps,),
            in_specs=[pl.BlockSpec((rows, block), lambda i, u: (0, i + first))]
            + ([] if earlier is None else [pl.BlockSpec(memory_space=pl.ANY)])
            + [pl.BlockSpec(h.shape, lambda i, u: (0, 0), pipeline_mode=pl.Buffered(1)) for h in halves]
            + [pl.BlockSpec((block, piece.shape[1]), lambda i, u: (i + first, 0)) for piece in pieces],
            out_specs=pl.BlockSpec((rows, block), lambda i, u: (0, i + first)),
            scratch_shapes=[pltpu.VMEM((rows, sum(widths)), jnp.bfloat16)],
        ),
        out_shape=jax.ShapeDtypeStruct(base.shape, kind),
        input_output_aliases={} if earlier is None else {2: 0},
        compiler_params=pltpu.CompilerParams(vmem_limit_bytes=VMEM_BYTES),
        cost_estimate=pl.CostEstimate(
            flops=2 * rows * steps * block * sum(widths),
            bytes_accessed=rows * steps * block * (base.dtype.itemsize + jnp.dtype(kind).itemsize),
            transcendentals=0,
        ),
    )(upper, base, *([] if earlier is None else [earlier]), *halves, *pieces)


def solution(mesh):
    rows, cols = mesh.shape["row"], mesh.shape["col"]

    def exchange(value, bit):
        return lax.ppermute(value, "col", [(i, i ^ bit) for i in range(cols)])

    def body(amplitudes, residual_in, cholesky):
        me = lax.axis_index("col")
        boxes = (me >> 20) == 0

        def boxed(run, *values):
            def never(*values):
                return jax.tree.map(lambda s: jnp.zeros(s.shape, s.dtype), jax.eval_shape(run, *values))

            return lax.cond(boxes, run, never, *values)

        bits = [1 << k for k in range(cols.bit_length() - 1)]
        upper = [(me & bit) != 0 for bit in bits]

        def split(value, step):
            low, high = jnp.split(value, 2)
            return jnp.where(upper[step], high, low), jnp.where(upper[step], low, high)

        def halve(value, step, kind):
            keep, send = split(value, step)
            return keep + exchange(send.astype(kind), bits[step]).astype(jnp.float32)

        def double(value, step):
            got = exchange(value, bits[step])
            mine = lax.broadcasted_iota(jnp.int32, (2, 1, 1), 0) == upper[step].astype(jnp.int32)
            return jnp.where(mine, value, got).reshape(2 * value.shape[0], value.shape[1])

        def finish(value):
            value = halve(halve(value, 2, jnp.float32), 3, jnp.float32).astype(jnp.bfloat16)
            return double(double(value, 3), 2)

        def both(value):
            return value, exchange(value, 1)

        flag = jnp.reshape(me & 1, (1,))
        mates = [[i for i in range(cols) if i % 2 == core] for core in range(2)]
        count = cols // 2

        def spread(value):
            return lax.all_to_all(value, "col", 0, 0, tiled=True, axis_index_groups=mates)

        def scatter(value):
            parts = spread(halve(value, 0, jnp.float32).astype(jnp.bfloat16)).astype(jnp.float32)
            return jnp.sum(parts.reshape(count, parts.shape[0] // count, -1), axis=0).astype(jnp.bfloat16)

        def gather(mine):
            return spread(jnp.tile(mine, (count, 1)))

        def chain(value):
            return gather(scatter(value))

        def last(quarter, part):
            mine = scatter(part)
            return both(after(double(quarter, 1), mine)), gather(mine)

        def send_row(vectors, shift):
            return lax.ppermute(vectors, "row", [(i, (i + shift) % rows) for i in range(rows)])

        if rows != 2 or len(bits) != 4 or sum(GROUPS) != cholesky.shape[1]:
            rest = jnp.concatenate([send_row(cholesky, shift) for shift in range(1, rows)], axis=1)
            pair = both(chain(project(amplitudes, cholesky)))
            total = project_back(residual_in, [pair], [cholesky], flag, jnp.float32)
            rest = after(rest, total)
            pair = both(chain(project(amplitudes, rest)))
            return project_back(total, [pair], [rest], flag, jnp.bfloat16)

        ends = [sum(GROUPS[: k + 1]) for k in range(len(GROUPS))]
        out_a, out_b, out_c = [cholesky[:, end - size : end] for end, size in zip(ends, GROUPS)]
        a = send_row(out_a, 1)
        part_own = project_wide(amplitudes, after(cholesky, out_a))
        keep, send = split(boxed(lambda v: halve(v, 0, jnp.float32), part_own), 1)
        got = exchange(send, bits[1])
        out_b = after(out_b, send)
        b = send_row(out_b, 1)
        part_a = project(amplitudes, after(a, out_b))
        quarter = boxed(finish, after(keep, part_a) + got)
        c = send_row(after(out_c, quarter), 1)
        part = jnp.concatenate([part_a, project(amplitudes, after(b, quarter))], axis=1)
        own, half_ab = boxed(last, quarter, part)
        pair_ab = both(half_ab)
        part_c = project(amplitudes, after(c, *pair_ab))

        def tail(part, residual, own, vectors):
            done = functools.partial(project_back, chis=[own], pieces=[vectors], upper=flag, kind=jnp.float32)
            total = done(residual, share=(0, 2))
            mine = after(scatter(part), total)
            total = done(after(residual, mine), share=(1, 2), earlier=total)
            return after(gather(mine), total), total

        half_c, total = boxed(tail, part_c, residual_in, own, cholesky)
        return project_back(total, [pair_ab, both(half_c)], [a, b, c], flag, jnp.bfloat16)

    in_specs = (P("row", "col"), P("row", "col"), P("col", "row"))
    return jax.shard_map(body, mesh=mesh, in_specs=in_specs, out_specs=P("row", "col"), check_vma=False)
```

```python
import functools

import jax
import jax.numpy as jnp
from jax import lax
from jax.experimental import pallas as pl
from jax.experimental.layout import Layout, with_layout_constraint
from jax.experimental.pallas import tpu as pltpu
from jax.sharding import PartitionSpec as P

GROUPS = (128, 256, 256)
VMEM_BYTES = 58 * 1024 * 1024
FREE = pl.CostEstimate(flops=0, bytes_accessed=0, transcendentals=0)


def after(value, *others):
    return lax.optimization_barrier((value, *others))[0]


def block_of(extent, target):
    while extent % target:
        target //= 2
    return target


def project(amplitudes, vectors):
    part = jnp.dot(amplitudes, vectors, preferred_element_type=jnp.float32)
    return with_layout_constraint(part, Layout(major_to_minor=(0, 1)))


def project_wide(amplitudes, vectors):
    rows, depth = amplitudes.shape
    width = vectors.shape[1]
    block = block_of(depth, 1024)
    steps = depth // block

    def kernel(left_ref, right_ref, out_ref, total_ref):
        step = pl.program_id(0)
        term = lax.dot_general(right_ref[...].T, left_ref[...], (((1,), (1,)), ((), ())), preferred_element_type=jnp.float32)

        @pl.when(step == 0)
        def _():
            total_ref[...] = term

        @pl.when((step > 0) & (step < steps - 1))
        def _():
            total_ref[...] += term

        @pl.when(step == steps - 1)
        def _():
            out_ref[...] = (total_ref[...] + term).T

    return pl.pallas_call(
        kernel,
        grid=(steps,),
        in_specs=[pl.BlockSpec((rows, block), lambda k: (0, k)), pl.BlockSpec((block, width), lambda k: (k, 0))],
        out_specs=pl.BlockSpec((rows, width), lambda k: (0, 0)),
        out_shape=jax.ShapeDtypeStruct((rows, width), jnp.float32),
        scratch_shapes=[pltpu.VMEM((width, rows), jnp.float32)],
        compiler_params=pltpu.CompilerParams(vmem_limit_bytes=VMEM_BYTES),
        cost_estimate=FREE,
    )(amplitudes, vectors)


def project_back(base, chis, pieces, upper, kind, share=(0, 1), earlier=None):
    rows, columns = base.shape
    block = block_of(columns // share[1], 1024)
    steps = columns // share[1] // block
    first = share[0] * steps
    half = rows // 2
    widths = [mine.shape[1] for mine, _ in chis]

    def kernel(upper_ref, base_ref, *refs):
        refs = refs if earlier is None else refs[1:]
        chi_refs, piece_refs, (out_ref, left_ref) = refs[: 2 * len(chis)], refs[2 * len(chis) : -2], refs[-2:]

        @pl.when(pl.program_id(0) == 0)
        def _():
            own = pl.multiple_of(upper_ref[0] * half, half)
            other = pl.multiple_of((1 - upper_ref[0]) * half, half)
            at = 0
            for k, width in enumerate(widths):
                left_ref[pl.ds(own, half), at : at + width] = chi_refs[2 * k][...]
                left_ref[pl.ds(other, half), at : at + width] = chi_refs[2 * k + 1][...]
                at += width

        right = jnp.concatenate([p[...] for p in piece_refs], axis=1)
        term = lax.dot_general(left_ref[...], right, (((1,), (1,)), ((), ())), preferred_element_type=jnp.float32)
        out_ref[...] = (base_ref[...].astype(jnp.float32) + term).astype(kind)

    halves = [h for pair in chis for h in pair]
    return pl.pallas_call(
        kernel,
        grid_spec=pltpu.PrefetchScalarGridSpec(
            num_scalar_prefetch=1,
            grid=(steps,),
            in_specs=[pl.BlockSpec((rows, block), lambda i, u: (0, i + first))]
            + ([] if earlier is None else [pl.BlockSpec(memory_space=pl.ANY)])
            + [pl.BlockSpec(h.shape, lambda i, u: (0, 0), pipeline_mode=pl.Buffered(1)) for h in halves]
            + [pl.BlockSpec((block, piece.shape[1]), lambda i, u: (i + first, 0)) for piece in pieces],
            out_specs=pl.BlockSpec((rows, block), lambda i, u: (0, i + first)),
            scratch_shapes=[pltpu.VMEM((rows, sum(widths)), jnp.bfloat16)],
        ),
        out_shape=jax.ShapeDtypeStruct(base.shape, kind),
        input_output_aliases={} if earlier is None else {2: 0},
        compiler_params=pltpu.CompilerParams(vmem_limit_bytes=VMEM_BYTES),
        cost_estimate=pl.CostEstimate(
            flops=2 * rows * steps * block * sum(widths),
            bytes_accessed=rows * steps * block * (base.dtype.itemsize + jnp.dtype(kind).itemsize),
            transcendentals=0,
        ),
    )(upper, base, *([] if earlier is None else [earlier]), *halves, *pieces)


def solution(mesh):
    rows, cols = mesh.shape["row"], mesh.shape["col"]

    def exchange(value, bit):
        return lax.ppermute(value, "col", [(i, i ^ bit) for i in range(cols)])

    def body(amplitudes, residual_in, cholesky):
        me = lax.axis_index("col")
        boxes = (me >> 20) == 0

        def boxed(run, *values):
            def never(*values):
                return jax.tree.map(lambda s: jnp.zeros(s.shape, s.dtype), jax.eval_shape(run, *values))

            return lax.cond(boxes, run, never, *values)

        bits = [1 << k for k in range(cols.bit_length() - 1)]
        upper = [(me & bit) != 0 for bit in bits]

        def split(value, step):
            low, high = jnp.split(value, 2)
            return jnp.where(upper[step], high, low), jnp.where(upper[step], low, high)

        def halve(value, step, kind):
            keep, send = split(value, step)
            return keep + exchange(send.astype(kind), bits[step]).astype(jnp.float32)

        def double(value, step):
            got = exchange(value, bits[step])
            mine = lax.broadcasted_iota(jnp.int32, (2, 1, 1), 0) == upper[step].astype(jnp.int32)
            return jnp.where(mine, value, got).reshape(2 * value.shape[0], value.shape[1])

        def finish(value):
            value = halve(halve(value, 2, jnp.bfloat16), 3, jnp.bfloat16).astype(jnp.bfloat16)
            return double(double(value, 3), 2)

        def both(value):
            return value, exchange(value, 1)

        flag = jnp.reshape(me & 1, (1,))
        mates = [[i for i in range(cols) if i % 2 == core] for core in range(2)]
        count = cols // 2

        def spread(value):
            return lax.all_to_all(value, "col", 0, 0, tiled=True, axis_index_groups=mates)

        def scatter(value):
            parts = spread(halve(value, 0, jnp.float32).astype(jnp.bfloat16)).astype(jnp.float32)
            return jnp.sum(parts.reshape(count, parts.shape[0] // count, -1), axis=0).astype(jnp.bfloat16)

        def gather(mine):
            return spread(jnp.tile(mine, (count, 1)))

        def chain(value):
            return gather(scatter(value))

        def send_row(vectors, shift):
            return lax.ppermute(vectors, "row", [(i, (i + shift) % rows) for i in range(rows)])

        if rows != 2 or len(bits) != 4 or sum(GROUPS) != cholesky.shape[1]:
            rest = jnp.concatenate([send_row(cholesky, shift) for shift in range(1, rows)], axis=1)
            pair = both(chain(project(amplitudes, cholesky)))
            total = project_back(residual_in, [pair], [cholesky], flag, jnp.float32)
            rest = after(rest, total)
            pair = both(chain(project(amplitudes, rest)))
            return project_back(total, [pair], [rest], flag, jnp.bfloat16)

        ends = [sum(GROUPS[: k + 1]) for k in range(len(GROUPS))]
        out_a, out_b, out_c = [cholesky[:, end - size : end] for end, size in zip(ends, GROUPS)]
        a = send_row(out_a, 1)
        part_own = project_wide(amplitudes, after(cholesky, out_a))
        keep, send = split(boxed(lambda v: halve(v, 0, jnp.float32), part_own), 1)
        got = exchange(send, bits[1])
        out_b = after(out_b, send)
        b = send_row(out_b, 1)
        part_a = project(amplitudes, after(a, out_b))
        quarter = boxed(finish, after(keep, part_a) + got)
        c = send_row(after(out_c, quarter), 1)
        half_own = double(quarter, 1)
        own = both(half_own)
        part = jnp.concatenate([part_a, project(amplitudes, after(b, half_own))], axis=1)

        def beside(part, residual, own, vectors):
            done = functools.partial(project_back, chis=[own], pieces=[vectors], upper=flag, kind=jnp.float32)
            total = done(residual, share=(0, 2))
            mine = after(scatter(part), total)
            total = done(after(residual, mine), share=(1, 2), earlier=total)
            return after(gather(mine), total), total

        half_ab, total = boxed(beside, part, residual_in, own, cholesky)
        pair_ab = both(half_ab)
        pair_c = both(chain(project(amplitudes, after(c, *pair_ab))))
        return project_back(total, [pair_ab, pair_c], [a, b, c], flag, jnp.bfloat16)

    in_specs = (P("row", "col"), P("row", "col"), P("col", "row"))
    return jax.shard_map(body, mesh=mesh, in_specs=in_specs, out_specs=P("row", "col"), check_vma=False)
```

```python
import functools

import jax
import jax.numpy as jnp
from jax import lax
from jax.experimental import pallas as pl
from jax.experimental.layout import Layout, with_layout_constraint
from jax.experimental.pallas import tpu as pltpu
from jax.sharding import PartitionSpec as P

GROUPS = (128, 256, 256)
VMEM_BYTES = 58 * 1024 * 1024
FREE = pl.CostEstimate(flops=0, bytes_accessed=0, transcendentals=0)


def after(value, *others):
    return lax.optimization_barrier((value, *others))[0]


def block_of(extent, target):
    while extent % target:
        target //= 2
    return target


def project(amplitudes, vectors):
    part = jnp.dot(amplitudes, vectors, preferred_element_type=jnp.float32)
    return with_layout_constraint(part, Layout(major_to_minor=(0, 1)))


def project_wide(amplitudes, vectors):
    rows, depth = amplitudes.shape
    width = vectors.shape[1]
    block = block_of(depth, 1024)
    steps = depth // block

    def kernel(left_ref, right_ref, out_ref, total_ref):
        step = pl.program_id(0)
        term = lax.dot_general(right_ref[...].T, left_ref[...], (((1,), (1,)), ((), ())), preferred_element_type=jnp.float32)

        @pl.when(step == 0)
        def _():
            total_ref[...] = term

        @pl.when((step > 0) & (step < steps - 1))
        def _():
            total_ref[...] += term

        @pl.when(step == steps - 1)
        def _():
            out_ref[...] = (total_ref[...] + term).T

    return pl.pallas_call(
        kernel,
        grid=(steps,),
        in_specs=[pl.BlockSpec((rows, block), lambda k: (0, k)), pl.BlockSpec((block, width), lambda k: (k, 0))],
        out_specs=pl.BlockSpec((rows, width), lambda k: (0, 0)),
        out_shape=jax.ShapeDtypeStruct((rows, width), jnp.float32),
        scratch_shapes=[pltpu.VMEM((width, rows), jnp.float32)],
        compiler_params=pltpu.CompilerParams(vmem_limit_bytes=VMEM_BYTES),
        cost_estimate=FREE,
    )(amplitudes, vectors)


def project_back(base, chis, pieces, upper, kind, share=(0, 1), earlier=None):
    rows, columns = base.shape
    block = block_of(columns // share[1], 1024)
    steps = columns // share[1] // block
    first = share[0] * steps
    half = rows // 2
    widths = [mine.shape[1] for mine, _ in chis]

    def kernel(upper_ref, base_ref, *refs):
        refs = refs if earlier is None else refs[1:]
        chi_refs, piece_refs, (out_ref, left_ref) = refs[: 2 * len(chis)], refs[2 * len(chis) : -2], refs[-2:]

        @pl.when(pl.program_id(0) == 0)
        def _():
            own = pl.multiple_of(upper_ref[0] * half, half)
            other = pl.multiple_of((1 - upper_ref[0]) * half, half)
            at = 0
            for k, width in enumerate(widths):
                left_ref[pl.ds(own, half), at : at + width] = chi_refs[2 * k][...]
                left_ref[pl.ds(other, half), at : at + width] = chi_refs[2 * k + 1][...]
                at += width

        right = jnp.concatenate([p[...] for p in piece_refs], axis=1)
        term = lax.dot_general(left_ref[...], right, (((1,), (1,)), ((), ())), preferred_element_type=jnp.float32)
        out_ref[...] = (base_ref[...].astype(jnp.float32) + term).astype(kind)

    halves = [h for pair in chis for h in pair]
    return pl.pallas_call(
        kernel,
        grid_spec=pltpu.PrefetchScalarGridSpec(
            num_scalar_prefetch=1,
            grid=(steps,),
            in_specs=[pl.BlockSpec((rows, block), lambda i, u: (0, i + first))]
            + ([] if earlier is None else [pl.BlockSpec(memory_space=pl.ANY)])
            + [pl.BlockSpec(h.shape, lambda i, u: (0, 0), pipeline_mode=pl.Buffered(1)) for h in halves]
            + [pl.BlockSpec((block, piece.shape[1]), lambda i, u: (i + first, 0)) for piece in pieces],
            out_specs=pl.BlockSpec((rows, block), lambda i, u: (0, i + first)),
            scratch_shapes=[pltpu.VMEM((rows, sum(widths)), jnp.bfloat16)],
        ),
        out_shape=jax.ShapeDtypeStruct(base.shape, kind),
        input_output_aliases={} if earlier is None else {2: 0},
        compiler_params=pltpu.CompilerParams(vmem_limit_bytes=VMEM_BYTES),
        cost_estimate=pl.CostEstimate(
            flops=2 * rows * steps * block * sum(widths),
            bytes_accessed=rows * steps * block * (base.dtype.itemsize + jnp.dtype(kind).itemsize),
            transcendentals=0,
        ),
    )(upper, base, *([] if earlier is None else [earlier]), *halves, *pieces)


def solution(mesh):
    rows, cols = mesh.shape["row"], mesh.shape["col"]

    def exchange(value, bit):
        return lax.ppermute(value, "col", [(i, i ^ bit) for i in range(cols)])

    def body(amplitudes, residual_in, cholesky):
        me = lax.axis_index("col")
        boxes = (me >> 20) == 0

        def boxed(run, *values):
            def never(*values):
                return jax.tree.map(lambda s: jnp.zeros(s.shape, s.dtype), jax.eval_shape(run, *values))

            return lax.cond(boxes, run, never, *values)

        bits = [1 << k for k in range(cols.bit_length() - 1)]
        upper = [(me & bit) != 0 for bit in bits]

        def split(value, step):
            low, high = jnp.split(value, 2)
            return jnp.where(upper[step], high, low), jnp.where(upper[step], low, high)

        def halve(value, step, kind):
            keep, send = split(value, step)
            return keep + exchange(send.astype(kind), bits[step]).astype(jnp.float32)

        def double(value, step):
            got = exchange(value, bits[step])
            mine = lax.broadcasted_iota(jnp.int32, (2, 1, 1), 0) == upper[step].astype(jnp.int32)
            return jnp.where(mine, value, got).reshape(2 * value.shape[0], value.shape[1])

        def finish(value):
            value = halve(halve(value, 2, jnp.bfloat16), 3, jnp.bfloat16).astype(jnp.bfloat16)
            return double(double(value, 3), 2)

        def both(value):
            return value, exchange(value, 1)

        flag = jnp.reshape(me & 1, (1,))
        mates = [[i for i in range(cols) if i % 2 == core] for core in range(2)]
        count = cols // 2

        def spread(value):
            return lax.all_to_all(value, "col", 0, 0, tiled=True, axis_index_groups=mates)

        def scatter(value):
            parts = spread(halve(value, 0, jnp.float32).astype(jnp.bfloat16)).astype(jnp.float32)
            return jnp.sum(parts.reshape(count, parts.shape[0] // count, -1), axis=0).astype(jnp.bfloat16)

        def gather(mine):
            return spread(jnp.tile(mine, (count, 1)))

        def chain(value):
            return gather(scatter(value))

        def send_row(vectors, shift):
            return lax.ppermute(vectors, "row", [(i, (i + shift) % rows) for i in range(rows)])

        if rows != 2 or len(bits) != 4 or sum(GROUPS) != cholesky.shape[1]:
            rest = jnp.concatenate([send_row(cholesky, shift) for shift in range(1, rows)], axis=1)
            pair = both(chain(project(amplitudes, cholesky)))
            total = project_back(residual_in, [pair], [cholesky], flag, jnp.float32)
            rest = after(rest, total)
            pair = both(chain(project(amplitudes, rest)))
            return project_back(total, [pair], [rest], flag, jnp.bfloat16)

        ends = [sum(GROUPS[: k + 1]) for k in range(len(GROUPS))]
        out_a, out_b, out_c = [cholesky[:, end - size : end] for end, size in zip(ends, GROUPS)]
        a = send_row(out_a, 1)
        part_own = project_wide(amplitudes, after(cholesky, out_a))
        keep, send = split(boxed(lambda v: halve(v, 0, jnp.float32), part_own), 1)
        got = exchange(send, bits[1])
        out_b = after(out_b, send)
        b = send_row(out_b, 1)
        part_a = project(amplitudes, after(a, out_b))
        quarter = boxed(finish, after(keep, part_a) + got)
        c = send_row(after(out_c, quarter), 1)
        half_own = double(quarter, 1)
        own = both(half_own)
        part = jnp.concatenate([part_a, project(amplitudes, after(b, half_own))], axis=1)

        def beside(part, residual, own, vectors):
            done = functools.partial(project_back, chis=[own], pieces=[vectors], upper=flag, kind=jnp.float32)
            total = done(residual, share=(0, 2))
            mine = after(scatter(part), total)
            total = done(after(residual, mine), share=(1, 2), earlier=total)
            return after(gather(mine), total), total

        half_ab, total = boxed(beside, part, residual_in, own, cholesky)
        pair_ab = both(half_ab)
        pair_c = both(chain(project(amplitudes, after(c, half_ab))))
        return project_back(total, [pair_ab, pair_c], [a, b, c], flag, jnp.bfloat16)

    in_specs = (P("row", "col"), P("row", "col"), P("col", "row"))
    return jax.shard_map(body, mesh=mesh, in_specs=in_specs, out_specs=P("row", "col"), check_vma=False)
```

```python
import functools

import jax
import jax.numpy as jnp
from jax import lax
from jax.experimental import pallas as pl
from jax.experimental.layout import Layout, with_layout_constraint
from jax.experimental.pallas import tpu as pltpu
from jax.sharding import PartitionSpec as P

GROUPS = (128, 256, 256)
VMEM_BYTES = 52 * 1024 * 1024
WIDE_VMEM_BYTES = 24 * 1024 * 1024
FREE = pl.CostEstimate(flops=0, bytes_accessed=0, transcendentals=0)


def after(value, *others):
    return lax.optimization_barrier((value, *others))[0]


def block_of(extent, target):
    while extent % target:
        target //= 2
    return target


def project(amplitudes, vectors):
    part = jnp.dot(amplitudes, vectors, preferred_element_type=jnp.float32)
    return with_layout_constraint(part, Layout(major_to_minor=(0, 1)))


def project_wide(amplitudes, vectors):
    rows, depth = amplitudes.shape
    width = vectors.shape[1]
    block = block_of(depth, 1024)
    steps = depth // block

    def kernel(left_ref, right_ref, out_ref, total_ref):
        step = pl.program_id(0)
        term = lax.dot_general(right_ref[...].T, left_ref[...], (((1,), (1,)), ((), ())), preferred_element_type=jnp.float32)

        @pl.when(step == 0)
        def _():
            total_ref[...] = term

        @pl.when((step > 0) & (step < steps - 1))
        def _():
            total_ref[...] += term

        @pl.when(step == steps - 1)
        def _():
            out_ref[...] = (total_ref[...] + term).T

    return pl.pallas_call(
        kernel,
        grid=(steps,),
        in_specs=[pl.BlockSpec((rows, block), lambda k: (0, k)), pl.BlockSpec((block, width), lambda k: (k, 0))],
        out_specs=pl.BlockSpec((rows, width), lambda k: (0, 0)),
        out_shape=jax.ShapeDtypeStruct((rows, width), jnp.float32),
        scratch_shapes=[pltpu.VMEM((width, rows), jnp.float32)],
        compiler_params=pltpu.CompilerParams(vmem_limit_bytes=WIDE_VMEM_BYTES),
        cost_estimate=FREE,
    )(amplitudes, vectors)


def project_back(base, chis, pieces, upper, kind, share=(0, 1), earlier=None):
    rows, columns = base.shape
    block = block_of(columns // share[1], 1024)
    steps = columns // share[1] // block
    first = share[0] * steps
    half = rows // 2
    widths = [mine.shape[1] for mine, _ in chis]

    def kernel(upper_ref, base_ref, *refs):
        refs = refs if earlier is None else refs[1:]
        chi_refs, piece_refs, (out_ref, left_ref) = refs[: 2 * len(chis)], refs[2 * len(chis) : -2], refs[-2:]

        @pl.when(pl.program_id(0) == 0)
        def _():
            own = pl.multiple_of(upper_ref[0] * half, half)
            other = pl.multiple_of((1 - upper_ref[0]) * half, half)
            at = 0
            for k, width in enumerate(widths):
                left_ref[pl.ds(own, half), at : at + width] = chi_refs[2 * k][...]
                left_ref[pl.ds(other, half), at : at + width] = chi_refs[2 * k + 1][...]
                at += width

        right = jnp.concatenate([p[...] for p in piece_refs], axis=1)
        term = lax.dot_general(left_ref[...], right, (((1,), (1,)), ((), ())), preferred_element_type=jnp.float32)
        out_ref[...] = (base_ref[...].astype(jnp.float32) + term).astype(kind)

    halves = [h for pair in chis for h in pair]
    return pl.pallas_call(
        kernel,
        grid_spec=pltpu.PrefetchScalarGridSpec(
            num_scalar_prefetch=1,
            grid=(steps,),
            in_specs=[pl.BlockSpec((rows, block), lambda i, u: (0, i + first))]
            + ([] if earlier is None else [pl.BlockSpec(memory_space=pl.ANY)])
            + [pl.BlockSpec(h.shape, lambda i, u: (0, 0), pipeline_mode=pl.Buffered(1)) for h in halves]
            + [pl.BlockSpec((block, piece.shape[1]), lambda i, u: (i + first, 0)) for piece in pieces],
            out_specs=pl.BlockSpec((rows, block), lambda i, u: (0, i + first)),
            scratch_shapes=[pltpu.VMEM((rows, sum(widths)), jnp.bfloat16)],
        ),
        out_shape=jax.ShapeDtypeStruct(base.shape, kind),
        input_output_aliases={} if earlier is None else {2: 0},
        compiler_params=pltpu.CompilerParams(vmem_limit_bytes=VMEM_BYTES),
        cost_estimate=pl.CostEstimate(
            flops=2 * rows * steps * block * sum(widths),
            bytes_accessed=rows * steps * block * (base.dtype.itemsize + jnp.dtype(kind).itemsize),
            transcendentals=0,
        ),
    )(upper, base, *([] if earlier is None else [earlier]), *halves, *pieces)


def solution(mesh):
    rows, cols = mesh.shape["row"], mesh.shape["col"]

    def exchange(value, bit):
        return lax.ppermute(value, "col", [(i, i ^ bit) for i in range(cols)])

    def body(amplitudes, residual_in, cholesky):
        me = lax.axis_index("col")
        boxes = (me >> 20) == 0

        def boxed(run, *values):
            def never(*values):
                return jax.tree.map(lambda s: jnp.zeros(s.shape, s.dtype), jax.eval_shape(run, *values))

            return lax.cond(boxes, run, never, *values)

        bits = [1 << k for k in range(cols.bit_length() - 1)]
        upper = [(me & bit) != 0 for bit in bits]

        def split(value, step):
            low, high = jnp.split(value, 2)
            return jnp.where(upper[step], high, low), jnp.where(upper[step], low, high)

        def halve(value, step, kind):
            keep, send = split(value, step)
            return keep + exchange(send.astype(kind), bits[step]).astype(jnp.float32)

        def double(value, step):
            got = exchange(value, bits[step])
            mine = lax.broadcasted_iota(jnp.int32, (2, 1, 1), 0) == upper[step].astype(jnp.int32)
            return jnp.where(mine, value, got).reshape(2 * value.shape[0], value.shape[1])

        def finish(value):
            value = halve(halve(value, 2, jnp.bfloat16), 3, jnp.bfloat16).astype(jnp.bfloat16)
            return double(double(value, 3), 2)

        def both(value):
            return value, exchange(value, 1)

        flag = jnp.reshape(me & 1, (1,))
        mates = [[i for i in range(cols) if i % 2 == core] for core in range(2)]
        count = cols // 2

        def spread(value):
            return lax.all_to_all(value, "col", 0, 0, tiled=True, axis_index_groups=mates)

        def scatter(value):
            parts = spread(halve(value, 0, jnp.float32).astype(jnp.bfloat16)).astype(jnp.float32)
            return jnp.sum(parts.reshape(count, parts.shape[0] // count, -1), axis=0).astype(jnp.bfloat16)

        def gather(mine):
            return spread(jnp.tile(mine, (count, 1)))

        def chain(value):
            return gather(scatter(value))

        def send_row(vectors, shift):
            return lax.ppermute(vectors, "row", [(i, (i + shift) % rows) for i in range(rows)])

        if rows != 2 or len(bits) != 4 or sum(GROUPS) != cholesky.shape[1]:
            rest = jnp.concatenate([send_row(cholesky, shift) for shift in range(1, rows)], axis=1)
            pair = both(chain(project(amplitudes, cholesky)))
            total = project_back(residual_in, [pair], [cholesky], flag, jnp.float32)
            rest = after(rest, total)
            pair = both(chain(project(amplitudes, rest)))
            return project_back(total, [pair], [rest], flag, jnp.bfloat16)

        ends = [sum(GROUPS[: k + 1]) for k in range(len(GROUPS))]
        out_a, out_b, out_c = [cholesky[:, end - size : end] for end, size in zip(ends, GROUPS)]
        a = send_row(out_a, 1)
        part_own = project_wide(amplitudes, after(cholesky, out_a))
        keep, send = split(boxed(lambda v: halve(v, 0, jnp.float32), part_own), 1)
        got = exchange(send, bits[1])
        out_b = after(out_b, send)
        b = send_row(out_b, 1)
        part_a = project(amplitudes, after(a, out_b))
        quarter = boxed(finish, after(keep, part_a) + got)
        c = send_row(after(out_c, quarter), 1)
        half_own = double(quarter, 1)
        own = both(half_own)
        part = jnp.concatenate([part_a, project(amplitudes, after(b, half_own))], axis=1)

        def beside(part, residual, own, vectors):
            done = functools.partial(project_back, chis=[own], pieces=[vectors], upper=flag, kind=jnp.float32)
            total = done(residual, share=(0, 2))
            mine = after(scatter(part), total)
            total = done(after(residual, mine), share=(1, 2), earlier=total)
            return after(gather(mine), total), total

        half_ab, total = boxed(beside, part, residual_in, own, cholesky)
        pair_ab = both(half_ab)
        pair_c = both(chain(project(amplitudes, after(c, half_ab))))
        return project_back(total, [pair_ab, pair_c], [a, b, c], flag, jnp.bfloat16)

    in_specs = (P("row", "col"), P("row", "col"), P("col", "row"))
    return jax.shard_map(body, mesh=mesh, in_specs=in_specs, out_specs=P("row", "col"), check_vma=False)
```

```python
import functools

import jax
import jax.numpy as jnp
from jax import lax
from jax.experimental import pallas as pl
from jax.experimental.layout import Layout, with_layout_constraint
from jax.experimental.pallas import tpu as pltpu
from jax.sharding import PartitionSpec as P

GROUPS = (128, 256, 256)
VMEM_BYTES = 52 * 1024 * 1024
WIDE_VMEM_BYTES = 58 * 1024 * 1024
FREE = pl.CostEstimate(flops=0, bytes_accessed=0, transcendentals=0)


def after(value, *others):
    return lax.optimization_barrier((value, *others))[0]


def block_of(extent, target):
    while extent % target:
        target //= 2
    return target


def project(amplitudes, vectors):
    part = jnp.dot(amplitudes, vectors, preferred_element_type=jnp.float32)
    return with_layout_constraint(part, Layout(major_to_minor=(0, 1)))


def project_wide(amplitudes, vectors):
    rows, depth = amplitudes.shape
    width = vectors.shape[1]
    block = block_of(depth, 1024)
    steps = depth // block

    def kernel(left_ref, right_ref, out_ref, total_ref):
        step = pl.program_id(0)
        term = lax.dot_general(right_ref[...].T, left_ref[...], (((1,), (1,)), ((), ())), preferred_element_type=jnp.float32)

        @pl.when(step == 0)
        def _():
            total_ref[...] = term

        @pl.when((step > 0) & (step < steps - 1))
        def _():
            total_ref[...] += term

        @pl.when(step == steps - 1)
        def _():
            out_ref[...] = (total_ref[...] + term).T

    return pl.pallas_call(
        kernel,
        grid=(steps,),
        in_specs=[pl.BlockSpec((rows, block), lambda k: (0, k)), pl.BlockSpec((block, width), lambda k: (k, 0))],
        out_specs=pl.BlockSpec((rows, width), lambda k: (0, 0)),
        out_shape=jax.ShapeDtypeStruct((rows, width), jnp.float32),
        scratch_shapes=[pltpu.VMEM((width, rows), jnp.float32)],
        compiler_params=pltpu.CompilerParams(vmem_limit_bytes=WIDE_VMEM_BYTES),
        cost_estimate=FREE,
    )(amplitudes, vectors)


def project_back(base, chis, pieces, upper, kind, share=(0, 1), earlier=None):
    rows, columns = base.shape
    block = block_of(columns // share[1], 1024)
    steps = columns // share[1] // block
    first = share[0] * steps
    half = rows // 2
    widths = [mine.shape[1] for mine, _ in chis]

    def kernel(upper_ref, base_ref, *refs):
        refs = refs if earlier is None else refs[1:]
        chi_refs, piece_refs, (out_ref, left_ref) = refs[: 2 * len(chis)], refs[2 * len(chis) : -2], refs[-2:]

        @pl.when(pl.program_id(0) == 0)
        def _():
            own = pl.multiple_of(upper_ref[0] * half, half)
            other = pl.multiple_of((1 - upper_ref[0]) * half, half)
            at = 0
            for k, width in enumerate(widths):
                left_ref[pl.ds(own, half), at : at + width] = chi_refs[2 * k][...]
                left_ref[pl.ds(other, half), at : at + width] = chi_refs[2 * k + 1][...]
                at += width

        right = jnp.concatenate([p[...] for p in piece_refs], axis=1)
        term = lax.dot_general(left_ref[...], right, (((1,), (1,)), ((), ())), preferred_element_type=jnp.float32)
        out_ref[...] = (base_ref[...].astype(jnp.float32) + term).astype(kind)

    halves = [h for pair in chis for h in pair]
    return pl.pallas_call(
        kernel,
        grid_spec=pltpu.PrefetchScalarGridSpec(
            num_scalar_prefetch=1,
            grid=(steps,),
            in_specs=[pl.BlockSpec((rows, block), lambda i, u: (0, i + first))]
            + ([] if earlier is None else [pl.BlockSpec(memory_space=pl.ANY)])
            + [pl.BlockSpec(h.shape, lambda i, u: (0, 0), pipeline_mode=pl.Buffered(1)) for h in halves]
            + [pl.BlockSpec((block, piece.shape[1]), lambda i, u: (i + first, 0)) for piece in pieces],
            out_specs=pl.BlockSpec((rows, block), lambda i, u: (0, i + first)),
            scratch_shapes=[pltpu.VMEM((rows, sum(widths)), jnp.bfloat16)],
        ),
        out_shape=jax.ShapeDtypeStruct(base.shape, kind),
        input_output_aliases={} if earlier is None else {2: 0},
        compiler_params=pltpu.CompilerParams(vmem_limit_bytes=VMEM_BYTES),
        cost_estimate=pl.CostEstimate(
            flops=2 * rows * steps * block * sum(widths),
            bytes_accessed=rows * steps * block * (base.dtype.itemsize + jnp.dtype(kind).itemsize),
            transcendentals=0,
        ),
    )(upper, base, *([] if earlier is None else [earlier]), *halves, *pieces)


def solution(mesh):
    rows, cols = mesh.shape["row"], mesh.shape["col"]

    def exchange(value, bit):
        return lax.ppermute(value, "col", [(i, i ^ bit) for i in range(cols)])

    def body(amplitudes, residual_in, cholesky):
        me = lax.axis_index("col")
        boxes = (me >> 20) == 0

        def boxed(run, *values):
            def never(*values):
                return jax.tree.map(lambda s: jnp.zeros(s.shape, s.dtype), jax.eval_shape(run, *values))

            return lax.cond(boxes, run, never, *values)

        bits = [1 << k for k in range(cols.bit_length() - 1)]
        upper = [(me & bit) != 0 for bit in bits]

        def split(value, step):
            low, high = jnp.split(value, 2)
            return jnp.where(upper[step], high, low), jnp.where(upper[step], low, high)

        def halve(value, step, kind):
            keep, send = split(value, step)
            return keep + exchange(send.astype(kind), bits[step]).astype(jnp.float32)

        def double(value, step):
            got = exchange(value, bits[step])
            mine = lax.broadcasted_iota(jnp.int32, (2, 1, 1), 0) == upper[step].astype(jnp.int32)
            return jnp.where(mine, value, got).reshape(2 * value.shape[0], value.shape[1])

        def finish(value):
            value = halve(halve(value, 2, jnp.bfloat16), 3, jnp.bfloat16).astype(jnp.bfloat16)
            return double(double(value, 3), 2)

        def both(value):
            return value, exchange(value, 1)

        flag = jnp.reshape(me & 1, (1,))
        mates = [[i for i in range(cols) if i % 2 == core] for core in range(2)]
        count = cols // 2

        def spread(value):
            return lax.all_to_all(value, "col", 0, 0, tiled=True, axis_index_groups=mates)

        def scatter(value):
            parts = spread(halve(value, 0, jnp.float32).astype(jnp.bfloat16)).astype(jnp.float32)
            return jnp.sum(parts.reshape(count, parts.shape[0] // count, -1), axis=0).astype(jnp.bfloat16)

        def gather(mine):
            return spread(jnp.tile(mine, (count, 1)))

        def chain(value):
            return gather(scatter(value))

        def send_row(vectors, shift):
            return lax.ppermute(vectors, "row", [(i, (i + shift) % rows) for i in range(rows)])

        if rows != 2 or len(bits) != 4 or sum(GROUPS) != cholesky.shape[1]:
            rest = jnp.concatenate([send_row(cholesky, shift) for shift in range(1, rows)], axis=1)
            pair = both(chain(project(amplitudes, cholesky)))
            total = project_back(residual_in, [pair], [cholesky], flag, jnp.float32)
            rest = after(rest, total)
            pair = both(chain(project(amplitudes, rest)))
            return project_back(total, [pair], [rest], flag, jnp.bfloat16)

        ends = [sum(GROUPS[: k + 1]) for k in range(len(GROUPS))]
        out_a, out_b, out_c = [cholesky[:, end - size : end] for end, size in zip(ends, GROUPS)]
        a = send_row(out_a, 1)
        part_own = project_wide(amplitudes, after(cholesky, out_a))
        keep, send = split(boxed(lambda v: halve(v, 0, jnp.float32), part_own), 1)
        got = exchange(send, bits[1])
        out_b = after(out_b, send)
        b = send_row(out_b, 1)
        part_a = project(amplitudes, after(a, out_b))
        quarter = boxed(finish, after(keep, part_a) + got)
        c = send_row(after(out_c, quarter), 1)
        half_own = double(quarter, 1)
        own = both(half_own)
        part = jnp.concatenate([part_a, project(amplitudes, after(b, half_own))], axis=1)

        def beside(part, residual, own, vectors):
            done = functools.partial(project_back, chis=[own], pieces=[vectors], upper=flag, kind=jnp.float32)
            total = done(residual, share=(0, 2))
            mine = after(scatter(part), total)
            total = done(after(residual, mine), share=(1, 2), earlier=total)
            return after(gather(mine), total), total

        half_ab, total = boxed(beside, part, residual_in, own, cholesky)
        pair_ab = both(half_ab)
        pair_c = both(chain(project(amplitudes, after(c, half_ab))))
        return project_back(total, [pair_ab, pair_c], [a, b, c], flag, jnp.bfloat16)

    in_specs = (P("row", "col"), P("row", "col"), P("col", "row"))
    return jax.shard_map(body, mesh=mesh, in_specs=in_specs, out_specs=P("row", "col"), check_vma=False)
```
